32 devices in a mesh: groups: 2 (over y), adapter: 4 (over z), tensor: 2 (over x), replica: 2 (over core).
Axes of the slice: x: 2, y: 2, z: 4, core: 2. Of those that a mesh axis runs over, the one named last changes fastest.
Arguments:
- hidden_state_rows: bfloat16 [8192, 8192], P(('groups', 'adapter', 'replica'), 'tensor'), parts along dimension 0, may hold values from -6 to 6
- value_matrix: bfloat16 [8192, 1024], P('tensor', 'replica'), may hold values from -0.0625 to 0.0625
- adapter_down_weight: bfloat16 [4, 8192, 64], P('adapter', 'tensor'), may hold values from -0.0625 to 0.0625
- adapter_up_weight: bfloat16 [4, 64, 1024], P('adapter', None, 'tensor'), may hold values from -0.75 to 0.75
- adapter_index_rows: int32 [8192, 1], P(('groups', 'adapter', 'replica')), parts along dimension 0, may hold values from 0 to 3; in each aligned block of 512 rows (0 to 511, 512 to 1023, ...) at most 256 rows name the same one
Outputs:
- values: bfloat16 [8192, 1024], P(('groups', 'adapter', 'replica'), 'tensor'), parts along dimension 0
The draws below stay inside these ranges and needn't reach their ends.
There are 2 independent parts, one for each index of `groups`. The reference program is written for one: setup_inputs(seed, part) draws one part's arguments, and reference() takes and returns one part's arrays. A program takes and returns all parts, laid end to end along the dimension named above; an argument that names none is the same for every part. Nothing has to cross between parts.
Inputs may be any that keep to these rules, and one draw needn't show every extreme that they name: `adapter_index_rows`: among the rows of one device (aligned blocks of 512 rows) no adapter is named by more than 256 rows; some adapter is named by exactly 256 rows of some device.
All inputs are finite; a program needn't handle non-finite values.
Results may differ from the reference program's by a relative error of at most 0.007.
Values may be sent and summed in bfloat16 or wider, within the bound.
No kernel may reach another device: no remote copies, remote signals or barrier semaphores. Data moves between devices by JAX's collectives and lax.ppermute only.
A program may use at most 128 MiB of HBM per device.

```python
import math
import jax
import jax.numpy as jnp
import numpy as np
from jax import lax

MODEL_WIDTH = 8192
ADAPTER_RANK = 64
TOK_DEV = 512
VALUE_FEATURES = 1024
ADAPTER_COUNT = 4
GROUP_ROWS = 4096
CAP = 256


def block_levels(rng, dims, split, smallest, top_value):
    loudness, own = 1.0, jax.random.fold_in(rng, 6)
    for axis_at, parts in split:
        draws = jnp.exp(jax.random.uniform(jax.random.fold_in(own, axis_at), (parts,), jnp.float32, smallest / len(split), top_value / len(split)))
        loudness = loudness * jnp.repeat(draws, dims[axis_at] // parts).reshape([-1 if axis == axis_at else 1 for axis in range(len(dims))])
    return loudness


def deal_out(own_key, own, number, rows, amount, top, limit, skew):
    sequence = jax.random.permutation(own_key, amount)
    packed, ordinary = load_shares(amount, rows * top, limit, skew, True), load_shares(amount, rows * top, limit, skew, False)
    places = jnp.arange(amount)

    def named(sizes, offset_by):
        used = int((sizes > 0).sum())
        fixed = max(1, used // 4)
        shifted = fixed + (places - fixed + offset_by * (used - fixed)) % max(1, amount - fixed)
        return jnp.zeros((amount,), jnp.int32).at[sequence[jnp.where(places < fixed, places, shifted)]].set(jnp.asarray(sizes, jnp.int32))

    sizes = jnp.where(number % 4 == 0, named(packed, number // 4), named(ordinary, number - number // 4 - 1))
    mixed = jax.random.permutation(jax.random.fold_in(own, 3), amount)
    giver, receiver = mixed[0:amount // 2 * 2:2], mixed[1:amount // 2 * 2:2]
    room = jnp.minimum(sizes[giver] - 1, limit - sizes[receiver]) // 2
    room = jnp.where((giver == sequence[0]) | (receiver == sequence[0]) | (sizes[receiver] == 0), 0, jnp.maximum(room, 0))
    shifted = jax.random.randint(jax.random.fold_in(own, 4), (amount // 2,), 0, 1 << 20) % (room + 1)
    sizes = sizes.at[giver].add(-shifted).at[receiver].add(shifted)
    items = jnp.searchsorted(jnp.cumsum(sizes), jnp.arange(rows * top), side="right").astype(jnp.int32)
    table = items.reshape(top, rows).T
    table = table[jax.random.permutation(jax.random.fold_in(own, 1), rows)]
    offset_by = jax.random.randint(jax.random.fold_in(own, 2), (rows, 1), 0, top)
    return jnp.take_along_axis(table, (jnp.arange(top)[None, :] + offset_by) % top, axis=1)


def load_shares(number_of, total, reach, lean, full):
    portions = [(1 << 20) // math.isqrt(grade ** lean) + 1 for grade in range(1, number_of + 1)]
    largest = reach if full else min(reach, max(-(-total // number_of), total * portions[0] // sum(portions)))
    least = 1 if total - largest >= number_of - 1 else 0
    given, surplus = [largest] + [least] * (number_of - 1), total - largest - least * (number_of - 1)
    while surplus > 0:
        movable = [i for i in range(1, number_of) if given[i] < largest] or [i for i in range(1, number_of) if given[i] < reach]
        mass, left = sum([portions[i] for i in movable]), surplus
        for i in movable:
            extra = min(reach - given[i], max(1, left * portions[i] // mass), surplus)
            given[i] = given[i] + extra
            surplus = surplus - extra
    return np.array(given)


def gaussian(own_key, dims, deviation, most, pieces=(), dtype=jnp.bfloat16):
    array = jax.random.normal(own_key, dims, jnp.float32) * deviation
    if len(pieces) > 0:
        array = block_levels(own_key, dims, pieces, -0.22, 0.18) * array
    return jnp.clip(array, min=-most, max=most).astype(dtype)


def setup_inputs(seed: int = 0, part: int = 0) -> dict:
    keys = jax.random.split(jax.random.key(seed), 6)
    part_keys = jax.random.split(jax.random.fold_in(keys[5], part), 6)
    hidden_state_rows = gaussian(part_keys[0], (GROUP_ROWS, MODEL_WIDTH), 1.0, 6.0, ((0, 8), (1, 2)))
    value_matrix = gaussian(keys[1], (MODEL_WIDTH, VALUE_FEATURES), MODEL_WIDTH ** -0.5, 0.0625, ((0, 2), (1, 2)))
    adapter_down_weight = gaussian(keys[2], (ADAPTER_COUNT, MODEL_WIDTH, ADAPTER_RANK), MODEL_WIDTH ** -0.5, 0.0625, ((0, 4), (1, 2)))
    adapter_up_weight = gaussian(keys[3], (ADAPTER_COUNT, ADAPTER_RANK, VALUE_FEATURES), ADAPTER_RANK ** -0.5, 0.75, ((0, 4), (2, 2)))
    adapter_index_rows_keys = jax.random.split(jax.random.fold_in(part_keys[4], 1), GROUP_ROWS // TOK_DEV)
    adapter_index_rows_turns = jax.random.permutation(jax.random.fold_in(part_keys[4], 3), GROUP_ROWS // TOK_DEV)
    adapter_index_rows = jax.vmap(lambda own, number: deal_out(jax.random.fold_in(part_keys[4], 2), own, number, TOK_DEV, ADAPTER_COUNT, 1, CAP, 2))(adapter_index_rows_keys, adapter_index_rows_turns).reshape((GROUP_ROWS, 1))
    return {"hidden_state_rows": hidden_state_rows, "value_matrix": value_matrix, "adapter_down_weight": adapter_down_weight, "adapter_up_weight": adapter_up_weight, "adapter_index_rows": adapter_index_rows}


def reference(hidden_state_rows, value_matrix, adapter_down_weight, adapter_up_weight, adapter_index_rows):
    base_output = jnp.dot(hidden_state_rows, value_matrix, preferred_element_type=jnp.float32)
    adapter_indices = adapter_index_rows[:, 0].astype(jnp.int32)
    adapter_block = 64
    def single_block(pair):
        rows, adapter_index = pair
        down_weight = adapter_down_weight[adapter_index].astype(jnp.float32)
        low = jnp.einsum("rd,rdq->rq", rows.astype(jnp.float32), down_weight)
        lowrank_state = lax.optimization_barrier(low.astype(jnp.bfloat16))
        up_weight = adapter_up_weight[adapter_index].astype(jnp.float32)
        adapter_output = jnp.einsum("sy,syf->sf", lowrank_state.astype(jnp.float32), up_weight)
        return adapter_output.astype(jnp.bfloat16)
    adapter_output = lax.map(single_block, (hidden_state_rows.reshape(-1, adapter_block, MODEL_WIDTH), adapter_indices.reshape(-1, adapter_block)))
    adapter_output = adapter_output.reshape(GROUP_ROWS, VALUE_FEATURES)
    return (base_output + adapter_output.astype(jnp.float32)).astype(jnp.bfloat16)
```

```python
import jax
import jax.numpy as jnp
from jax import lax
from jax.sharding import PartitionSpec as P

F32 = jnp.float32
BF16 = jnp.bfloat16


def shift(x, axis, size, by):
    return lax.ppermute(x, axis, [(i, (i + by) % size) for i in range(size)])


def build(mesh):
    groups, adapters = mesh.shape["groups"], mesh.shape["adapter"]
    tensors, replicas = mesh.shape["tensor"], mesh.shape["replica"]

    def others(x, axis, size):
        return [shift(x, axis, size, by) for by in range(1, size)]

    def shards(x, v, d, u, idx):
        g, a = lax.axis_index("groups"), lax.axis_index("adapter")
        t, r = lax.axis_index("tensor"), lax.axis_index("replica")
        rank, wide = d.shape[2], d.shape[1]
        cols, width = u.shape[2], v.shape[1]
        per = width // cols if width >= cols else 1

        held = [v] + others(v, "replica", replicas)

        own = jnp.concatenate([d[0].T, u[0]], axis=1)
        share = rank // (groups * replicas)
        mine = lax.dynamic_slice_in_dim(own, (g * replicas + r) * share, share, 0)
        down, up = [d[0].T], [u[0]]
        for by in range(1, adapters):
            part = shift(mine, "adapter", adapters, by)
            parts = jnp.concatenate([part] + others(part, "groups", groups), axis=0)
            parts = jnp.concatenate([parts] + others(parts, "replica", replicas), axis=0)
            down.append(parts[:, :wide])
            up.append(parts[:, wide:])

        local = jnp.zeros((x.shape[0], cols), F32)
        for h in range(replicas):
            terms = jnp.dot(x, held[h], preferred_element_type=F32)
            half = lax.rem(r - h + replicas, replicas)
            first = half * per
            here = (t >= first) & (t < first + per)
            block = lax.dynamic_slice_in_dim(terms, jnp.clip(t - first, 0, per - 1) * cols, cols, 1)
            local = local + jnp.where(here, block, 0.0)
            for by in range(1, tensors):
                pairs = [
                    (ti * replicas + ri, (ti + by) % tensors * replicas + ri)
                    for ti in range(tensors)
                    for ri in range(replicas)
                    if ((ti + by) % tensors) // per == (ri - h) % replicas
                ]
                if not pairs:
                    continue
                to = lax.rem(t + by, tensors)
                block = lax.dynamic_slice_in_dim(
                    terms, jnp.clip(to - first, 0, per - 1) * cols, cols, 1
                ).astype(BF16)
                local = local + lax.ppermute(block, ("tensor", "replica"), pairs).astype(F32)

        owner = lax.rem(a - jnp.arange(adapters, dtype=jnp.int32) + adapters, adapters)
        match = idx == owner[None, :]
        prod = jnp.einsum(
            "rd,qd->rq", x, jnp.concatenate(down, axis=0), preferred_element_type=F32
        ).reshape(x.shape[0], adapters, rank)
        low = jnp.sum(jnp.where(match[:, :, None], prod, 0.0), axis=1)
        sent = low.astype(BF16)
        low = low + sum(o.astype(F32) for o in others(sent, "tensor", tensors))
        low = low.astype(BF16)
        spread = jnp.where(match[:, :, None], low[:, None, :], 0).reshape(x.shape[0], adapters * rank)
        lora = jnp.dot(spread, jnp.concatenate(up, axis=0), preferred_element_type=F32).astype(BF16)
        return (local + lora.astype(F32)).astype(BF16)

    return shards


def solution(mesh):
    return jax.shard_map(
        build(mesh),
        mesh=mesh,
        in_specs=(
            P(("groups", "adapter", "replica"), "tensor"),
            P("tensor", "replica"),
            P("adapter", "tensor", None),
            P("adapter", None, "tensor"),
            P(("groups", "adapter", "replica"), None),
        ),
        out_specs=P(("groups", "adapter", "replica"), "tensor"),
        check_vma=False,
    )
```

```python
import functools

import jax
import jax.numpy as jnp
from jax import lax
from jax.experimental import pallas as pl
from jax.experimental.pallas import tpu as pltpu
from jax.sharding import PartitionSpec as P

F32 = jnp.float32
BF16 = jnp.bfloat16
VMEM = pl.BlockSpec(memory_space=pltpu.VMEM)
SMEM = pl.BlockSpec(memory_space=pltpu.SMEM)
BATCH = 4


def call(kernel, outs, args, scratch=(), flops=0, limit=16, specs=None):
    size = sum(a.size * a.dtype.itemsize for a in args)
    return pl.pallas_call(
        kernel,
        out_shape=outs,
        in_specs=specs or [VMEM] * len(args),
        out_specs=jax.tree.map(lambda _: VMEM, outs),
        scratch_shapes=scratch,
        compiler_params=pltpu.CompilerParams(vmem_limit_bytes=limit << 20),
        cost_estimate=pl.CostEstimate(flops=flops, bytes_accessed=size, transcendentals=0),
    )(*args)


def base_kernel(x_ref, v_ref, o_ref):
    o_ref[...] = jnp.dot(x_ref[...], v_ref[...], preferred_element_type=F32).astype(BF16)


def base_terms(x, v):
    out = jax.ShapeDtypeStruct((x.shape[0], v.shape[1]), BF16)
    return call(base_kernel, out, (x, v), flops=2 * x.size * v.shape[1])


def fill(scratch, group, lanes):
    row = 0
    for parts in group:
        for part in parts:
            scratch[row : row + part.shape[0], :] = part[:, lanes]
            row += part.shape[0]
    return row


def down_kernel(layout, wide, owner_ref, idx_ref, x_ref, *refs):
    parts, (low_ref, sent_ref, scratch) = refs[:-3], refs[-3:]
    groups, at = [], 0
    for count in layout:
        groups.append(parts[at : at + count])
        at += count
    rank = low_ref.shape[0]
    low = jnp.zeros(low_ref.shape, F32)
    for first in range(0, len(groups), BATCH):
        group = groups[first : first + BATCH]
        rows = fill(scratch, group, slice(0, wide))
        prod = lax.dot_general(
            scratch[:rows, :], x_ref[...], (((1,), (1,)), ((), ())), preferred_element_type=F32
        )
        for k in range(len(group)):
            match = idx_ref[...] == owner_ref[first + k]
            low = low + jnp.where(match, prod[k * rank : (k + 1) * rank, :], 0.0)
    low_ref[...] = low
    sent_ref[...] = low.astype(BF16)


def last_kernel(layout, wide, owner_ref, here_ref, idx_ref, low_ref, *refs):
    counts, refs = layout, list(refs)
    take = lambda n: [refs.pop(0) for _ in range(n)]
    lows, parts = take(counts[0]), take(sum(counts[1]))
    blocks, recvs = take(counts[2]), take(counts[3])
    out_ref, up, spread = refs
    groups, at = [], 0
    for count in counts[1]:
        groups.append(parts[at : at + count])
        at += count
    rank, cols = low_ref.shape[0], out_ref.shape[1]
    low = low_ref[...]
    for other in lows:
        low = low + other[...].astype(F32)
    low = low.astype(BF16).astype(F32)
    lora = jnp.zeros(out_ref.shape, F32)
    for first in range(0, len(groups), BATCH):
        group = groups[first : first + BATCH]
        row = 0
        for k, members in enumerate(group):
            match = idx_ref[...] == owner_ref[first + k]
            spread[k * rank : (k + 1) * rank, :] = jnp.where(match, low, 0.0).astype(BF16)
            for part in members:
                begin = part.shape[1] - cols
                up[row : row + part.shape[0], :] = part[:, begin : begin + cols]
                row += part.shape[0]
        lora = lora + lax.dot_general(
            spread[:row, :], up[:row, :], (((0,), (0,)), ((), ())), preferred_element_type=F32
        )
    total = lora.astype(BF16).astype(F32)
    for recv in recvs:
        total = total + recv[...].astype(F32)
    for h, block in enumerate(blocks):
        total = total + jnp.where(here_ref[h] == 1, block[...].astype(F32), 0.0)
    out_ref[...] = total.astype(BF16)


def shift(x, axis, size, by):
    return lax.ppermute(x, axis, [(i, (i + by) % size) for i in range(size)])


def after(x, *others):
    return lax.optimization_barrier((x, *others))[0]


def build(mesh):
    groups, adapters = mesh.shape["groups"], mesh.shape["adapter"]
    tensors, replicas = mesh.shape["tensor"], mesh.shape["replica"]

    def others(x, axis, size):
        return [shift(x, axis, size, by) for by in range(1, size)]

    def shards(x, v, d, u, idx):
        g, a = lax.axis_index("groups"), lax.axis_index("adapter")
        t, r = lax.axis_index("tensor"), lax.axis_index("replica")
        tokens, rank, wide = x.shape[0], d.shape[2], d.shape[1]
        cols, width = u.shape[2], v.shape[1]
        per = width // cols
        row = idx.reshape(1, tokens)
        owner = lax.rem(a - jnp.arange(adapters, dtype=jnp.int32) + adapters, adapters)

        held = [v] + others(v, "replica", replicas)

        down = d[0].T
        own = jnp.concatenate([down, u[0]], axis=1)
        share = rank // (groups * replicas)
        mine = lax.dynamic_slice_in_dim(own, (g * replicas + r) * share, share, 0)
        first = [shift(mine, "adapter", adapters, by) for by in range(1, adapters)]

        blocks, recvs, here = [], [], []
        for h in range(replicas):
            terms = base_terms(x, held[h])
            half = lax.rem(r - h + replicas, replicas)
            begin = half * per

            def cut(n):
                if per == 1:
                    return terms
                at = jnp.clip(n - begin, 0, per - 1) * cols
                return lax.dynamic_slice_in_dim(terms, at, cols, 1)

            blocks.append(cut(t))
            here.append(((t >= begin) & (t < begin + per)).astype(jnp.int32))
            for by in range(1, tensors):
                pairs = [
                    (ti * replicas + ri, (ti + by) % tensors * replicas + ri)
                    for ti in range(tensors)
                    for ri in range(replicas)
                    if ((ti + by) % tensors) // per == (ri - h) % replicas
                ]
                if pairs:
                    block = cut(lax.rem(t + by, tensors))
                    recvs.append(lax.ppermute(block, ("tensor", "replica"), pairs))

        parts = []
        for part in first:
            members = [part] + others(part, "groups", groups)
            both = jnp.concatenate(members, axis=0) if groups > 1 else part
            members += others(both, "replica", replicas)
            parts.append(members)

        layout = [1] + [len(members) for members in parts]
        refs = [ref for members in parts for ref in members]
        low, sent = call(
            functools.partial(down_kernel, layout, wide),
            (jax.ShapeDtypeStruct((rank, tokens), F32), jax.ShapeDtypeStruct((rank, tokens), BF16)),
            (owner, row, x, down, *refs),
            scratch=[pltpu.VMEM((min(BATCH, adapters) * rank, wide), BF16)],
            flops=2 * x.size * rank * adapters,
            specs=[SMEM] + [VMEM] * (3 + len(refs)),
        )
        lows = others(sent, "tensor", tensors)
        return call(
            functools.partial(last_kernel, (len(lows), layout, len(blocks), len(recvs)), wide),
            jax.ShapeDtypeStruct((tokens, cols), BF16),
            (owner, jnp.stack(here), row, low, *lows, u[0], *refs, *blocks, *recvs),
            scratch=[
                pltpu.VMEM((min(BATCH, adapters) * rank, cols), BF16),
                pltpu.VMEM((min(BATCH, adapters) * rank, tokens), BF16),
            ],
            flops=2 * tokens * rank * adapters * cols,
            specs=[SMEM] * 2 + [VMEM] * (3 + len(lows) + len(refs) + len(blocks) + len(recvs)),
        )

    return shards


def solution(mesh):
    return jax.shard_map(
        build(mesh),
        mesh=mesh,
        in_specs=(
            P(("groups", "adapter", "replica"), "tensor"),
            P("tensor", "replica"),
            P("adapter", "tensor", None),
            P("adapter", None, "tensor"),
            P(("groups", "adapter", "replica"), None),
        ),
        out_specs=P(("groups", "adapter", "replica"), "tensor"),
        check_vma=False,
    )
```

```python
import functools

import jax
import jax.numpy as jnp
from jax import lax
from jax.experimental import pallas as pl
from jax.experimental.pallas import tpu as pltpu
from jax.sharding import PartitionSpec as P

F32 = jnp.float32
BF16 = jnp.bfloat16
VMEM = pl.BlockSpec(memory_space=pltpu.VMEM)
SMEM = pl.BlockSpec(memory_space=pltpu.SMEM)
HBM = pl.BlockSpec(memory_space=pltpu.HBM)
WHOLE = 58
CHUNKS = 4
BATCH = 4


def call(kernel, outs, args, scratch=(), flops=0, limit=16, specs=None):
    size = sum(a.size * a.dtype.itemsize for a in args)
    return pl.pallas_call(
        kernel,
        out_shape=outs,
        in_specs=specs or [VMEM] * len(args),
        out_specs=jax.tree.map(lambda _: VMEM, outs),
        scratch_shapes=scratch,
        compiler_params=pltpu.CompilerParams(vmem_limit_bytes=limit << 20),
        cost_estimate=pl.CostEstimate(flops=flops, bytes_accessed=size, transcendentals=0),
    )(*args)


def chunks(refs, buffers, sems):
    copies = []
    for k in range(CHUNKS):
        copies.append([])
        for n, (ref, buffer) in enumerate(zip(refs, buffers)):
            copy = pltpu.make_async_copy(ref(k), buffer.at[k], sems.at[n, k])
            copy.start()
            copies[-1].append(copy)
    return copies


def part(ref, axis):
    size = ref.shape[axis] // CHUNKS
    if axis == 0:
        return lambda k: ref.at[pl.ds(k * size, size)]
    return lambda k: ref.at[:, pl.ds(k * size, size)]


def base_kernel(x_ref, v_ref, o_ref, x_buf, v_buf, acc, sems):
    copies = chunks((part(x_ref, 1), part(v_ref, 0)), (x_buf, v_buf), sems)
    for k in range(CHUNKS):
        for copy in copies[k]:
            copy.wait()
        prod = jnp.dot(x_buf[k], v_buf[k], preferred_element_type=F32)
        if k > 0:
            prod = prod + acc[...]
        if k < CHUNKS - 1:
            acc[...] = prod
        else:
            o_ref[...] = prod.astype(BF16)


def base_terms(x, v):
    rows, wide, width = x.shape[0], x.shape[1], v.shape[1]
    return call(
        base_kernel,
        jax.ShapeDtypeStruct((rows, width), BF16),
        (x, v),
        scratch=[
            pltpu.VMEM((CHUNKS, rows, wide // CHUNKS), BF16),
            pltpu.VMEM((CHUNKS, wide // CHUNKS, width), BF16),
            pltpu.VMEM((rows, width), F32),
            pltpu.SemaphoreType.DMA((2, CHUNKS)),
        ],
        flops=2 * x.size * width,
        limit=WHOLE,
        specs=[HBM] * 2,
    )


def fill(scratch, refs, pieces, lanes):
    row = 0
    for which, begin, rows in pieces:
        scratch[row : row + rows, :] = refs[which][begin : begin + rows, lanes]
        row += rows


def down_kernel(layout, owner_ref, idx_ref, x_ref, own_ref, *refs):
    parts, (low_ref, sent_ref, up_ref, scratch, x_buf, acc, sems) = refs[:-7], refs[-7:]
    rank, wide, cols = low_ref.shape[0], x_ref.shape[1], own_ref.shape[1]
    copies = chunks((part(x_ref, 1),), (x_buf,), sems)
    up_ref[:rank, :] = own_ref[...]
    pieces = [p for pieces in layout[1:] for p in pieces]
    fill(up_ref.at[rank:], parts, pieces, slice(wide, wide + cols))
    low = jnp.zeros(low_ref.shape, F32)
    for first in range(0, len(layout), BATCH):
        group = layout[first : first + BATCH]
        rows = len(group) * rank
        for k in range(CHUNKS):
            lanes = slice(k * wide // CHUNKS, (k + 1) * wide // CHUNKS)
            fill(scratch.at[k], parts, [p for pieces in group for p in pieces], lanes)
            if first == 0:
                copies[k][0].wait()
            prod = lax.dot_general(
                scratch[k, :rows, :],
                x_buf[k],
                (((1,), (1,)), ((), ())),
                preferred_element_type=F32,
            )
            if k > 0:
                prod = prod + acc[:rows, :]
            if k < CHUNKS - 1:
                acc[:rows, :] = prod
        for k in range(len(group)):
            match = idx_ref[...] == owner_ref[first + k]
            low = low + jnp.where(match, prod[k * rank : (k + 1) * rank, :], 0.0)
    low_ref[...] = low
    sent_ref[...] = low.astype(BF16)


def last_kernel(blocks, owner_ref, flag_ref, idx_ref, low_ref, up_ref, *refs):
    terms, others, (out_ref, spread) = refs[:blocks], refs[blocks:-2], refs[-2:]
    rank = low_ref.shape[0]
    low = low_ref[...]
    for other in others:
        low = low + other[...].astype(F32)
    low = low.astype(BF16).astype(F32)
    for k in range(up_ref.shape[0] // rank):
        match = idx_ref[...] == owner_ref[k]
        spread[k * rank : (k + 1) * rank, :] = jnp.where(match, low, 0.0).astype(BF16)
    lora = lax.dot_general(
        spread[...], up_ref[...], (((0,), (0,)), ((), ())), preferred_element_type=F32
    )
    total = lora.astype(BF16).astype(F32)
    for n, term in enumerate(terms):
        total = total + jnp.where(flag_ref[n] == 1, term[...].astype(F32), 0.0)
    out_ref[...] = total.astype(BF16)


def after(x, *others):
    return lax.optimization_barrier((x, *others))[0]


def build(mesh):
    groups, adapters = mesh.shape["groups"], mesh.shape["adapter"]
    tensors, replicas = mesh.shape["tensor"], mesh.shape["replica"]

    def shift(x, axis, by):
        size = mesh.shape[axis]
        return lax.ppermute(x, axis, [(i, (i + by) % size) for i in range(size)])

    def others(x, axis):
        return [shift(x, axis, by) for by in range(1, mesh.shape[axis])]

    def flip(x, bit):
        return lax.ppermute(x, "adapter", [(i, i ^ bit) for i in range(adapters)])

    def base_pairs(h, by):
        pairs = {}
        for ti in range(tensors):
            for ri in range(replicas):
                to = (ti + by) % tensors
                if to // per_half == (ri - h) % replicas:
                    pairs[ti * replicas + ri] = to * replicas + ri
        free = set(range(tensors * replicas)) - set(pairs.values())
        for source in range(tensors * replicas):
            if source not in pairs:
                chip = source // replicas
                near = [n for n in sorted(free) if n // replicas == chip] or sorted(free)
                pairs[source] = near[0]
                free.remove(near[0])
        return sorted(pairs.items())

    per_half = max(1, tensors // replicas)

    def shards(x, v, d, u, idx):
        g, a = lax.axis_index("groups"), lax.axis_index("adapter")
        t, r = lax.axis_index("tensor"), lax.axis_index("replica")
        tokens, rank, wide = x.shape[0], d.shape[2], d.shape[1]
        cols = u.shape[2]
        row = idx.reshape(1, tokens)

        held = [v] + others(v, "replica")

        down = d[0].T
        own = jnp.concatenate([down, u[0]], axis=1)
        share = rank // (groups * replicas)
        mine = lax.dynamic_slice_in_dim(own, (g * replicas + r) * share, share, 0)
        bits = [1 << n for n in reversed(range((adapters - 1).bit_length()))]
        pieces, direct = {}, []
        for bit in bits:
            direct.append((bit, flip(mine, bit)))

        blocks, here, recvs, real = [], [], [], []

        def base(h):
            terms = base_terms(x, held[h])
            half = lax.rem(r - h + replicas, replicas)
            begin = half * per_half

            def cut(n):
                if per_half == 1:
                    return terms
                at = jnp.clip(n - begin, 0, per_half - 1) * cols
                return lax.dynamic_slice_in_dim(terms, at, cols, 1)

            blocks.append(cut(t))
            here.append((t >= begin) & (t < begin + per_half))
            for by in range(1, tensors):
                block = cut(lax.rem(t + by, tensors))
                if h == 0 and direct:
                    block = after(block, *[piece for _, piece in direct])
                recvs.append(lax.ppermute(block, ("tensor", "replica"), base_pairs(h, by)))
                real.append(here[-1])
            return terms

        x = after(x, mine)
        terms = base(0)
        for bit, piece in direct:
            pieces[bit] = after(piece, terms)
            for prior in [p for p in pieces if p > bit and not p & bit]:
                pieces[prior | bit] = flip(pieces[prior], bit)
        early = list(recvs)
        order = [p for p in sorted(pieces, key=lambda p: (bin(p).count("1"), p))]
        for h in range(1, replicas):
            terms = base(h)
        arrays, layout = [], [[(0, 0, rank)]]

        def keep(array):
            arrays.append(array)
            return len(arrays)

        near, places = [], []
        for p in order:
            piece = after(pieces[p], terms) if p == order[-1] else pieces[p]
            layout.append([])
            members = [piece] + others(piece, "groups")
            last = members.pop() if p == order[-1] and groups > 1 else None
            for member in members:
                layout[-1].append((keep(member), 0, share))
                places.append((len(layout) - 1, len(near)))
                near.append(member)
        if replicas > 1:
            for other in others(jnp.concatenate(list(lax.optimization_barrier((terms, *near, *early)))[1 : len(near) + 1], axis=0), "replica"):
                which = keep(other)
                for k, at in places:
                    layout[k].append((which, at * share, share))
        if last is not None:
            for member in [last] + others(last, "replica"):
                layout[-1].append((keep(member), 0, share))

        owner = jnp.stack([a] + [lax.bitwise_xor(a, jnp.int32(p)) for p in order])
        low, sent, every = call(
            functools.partial(down_kernel, layout),
            (jax.ShapeDtypeStruct((rank, tokens), F32), jax.ShapeDtypeStruct((rank, tokens), BF16),
                jax.ShapeDtypeStruct((adapters * rank, cols), BF16)),
            (owner, row, after(x, *recvs), u[0], down, *arrays),
            scratch=[
                pltpu.VMEM((CHUNKS, min(BATCH, adapters) * rank, wide // CHUNKS), BF16),
                pltpu.VMEM((CHUNKS, tokens, wide // CHUNKS), BF16),
                pltpu.VMEM((min(BATCH, adapters) * rank, tokens), F32),
                pltpu.SemaphoreType.DMA((1, CHUNKS)),
            ],
            flops=2 * x.size * rank * adapters,
            limit=WHOLE,
            specs=[SMEM, VMEM, HBM] + [VMEM] * (2 + len(arrays)),
        )
        lows = others(sent, "tensor")
        flags = jnp.stack(here + real).astype(jnp.int32)
        terms = blocks + recvs
        return call(
            functools.partial(last_kernel, len(terms)),
            jax.ShapeDtypeStruct((tokens, cols), BF16),
            (owner, flags, row, low, every, *terms, *lows),
            scratch=[pltpu.VMEM((adapters * rank, tokens), BF16)],
            flops=2 * tokens * rank * adapters * cols,
            specs=[SMEM] * 2 + [VMEM] * (3 + len(terms) + len(lows)),
        )

    return shards


def solution(mesh):
    return jax.shard_map(
        build(mesh),
        mesh=mesh,
        in_specs=(
            P(("groups", "adapter", "replica"), "tensor"),
            P("tensor", "replica"),
            P("adapter", "tensor", None),
            P("adapter", None, "tensor"),
            P(("groups", "adapter", "replica"), None),
        ),
        out_specs=P(("groups", "adapter", "replica"), "tensor"),
        check_vma=False,
    )
```

```python
import functools

import jax
import jax.numpy as jnp
from jax import lax
from jax.experimental import pallas as pl
from jax.experimental.pallas import tpu as pltpu
from jax.sharding import PartitionSpec as P

F32 = jnp.float32
BF16 = jnp.bfloat16
VMEM = pl.BlockSpec(memory_space=pltpu.VMEM)
SMEM = pl.BlockSpec(memory_space=pltpu.SMEM)
HBM = pl.BlockSpec(memory_space=pltpu.HBM)
CHUNKS = 4
BATCH = 4


def call(kernel, outs, args, scratch=(), flops=0, limit=16, specs=None):
    size = sum(a.size * a.dtype.itemsize for a in args)
    return pl.pallas_call(
        kernel,
        out_shape=outs,
        in_specs=specs or [VMEM] * len(args),
        out_specs=jax.tree.map(lambda _: VMEM, outs),
        scratch_shapes=scratch,
        compiler_params=pltpu.CompilerParams(vmem_limit_bytes=limit << 20),
        cost_estimate=pl.CostEstimate(flops=flops, bytes_accessed=size, transcendentals=0),
    )(*args)


def chunks(refs, buffers, sems):
    copies = []
    for k in range(CHUNKS):
        copies.append([])
        for n, (ref, buffer) in enumerate(zip(refs, buffers)):
            copy = pltpu.make_async_copy(ref(k), buffer.at[k], sems.at[n, k])
            copy.start()
            copies[-1].append(copy)
    return copies


def part(ref, axis):
    size = ref.shape[axis] // CHUNKS
    if axis == 0:
        return lambda k: ref.at[pl.ds(k * size, size)]
    return lambda k: ref.at[:, pl.ds(k * size, size)]


def add_chunk(k, prod, acc, out_ref):
    if k > 0:
        prod = prod + acc[...]
    if k < CHUNKS - 1:
        acc[...] = prod
    else:
        out_ref[...] = prod.astype(BF16)


def first_kernel(x_ref, v_ref, o_ref, x_out, v_buf, acc, sems):
    copies = chunks((part(x_ref, 1), part(v_ref, 0)), (x_out, v_buf), sems)
    for k in range(CHUNKS):
        for copy in copies[k]:
            copy.wait()
        add_chunk(k, jnp.dot(x_out[k], v_buf[k], preferred_element_type=F32), acc, o_ref)


def first_terms(x, v):
    rows, wide, width = x.shape[0], x.shape[1], v.shape[1]
    cut = (CHUNKS, rows, wide // CHUNKS)
    return call(
        first_kernel,
        (jax.ShapeDtypeStruct((rows, width), BF16), jax.ShapeDtypeStruct(cut, BF16)),
        (x, v),
        scratch=[
            pltpu.VMEM((CHUNKS, wide // CHUNKS, width), BF16),
            pltpu.VMEM((rows, width), F32),
            pltpu.SemaphoreType.DMA((2, CHUNKS)),
        ],
        flops=2 * x.size * width,
        limit=48,
        specs=[HBM] * 2,
    )


def next_kernel(x_ref, v_ref, o_ref, acc):
    size = x_ref.shape[2]
    for k in range(CHUNKS):
        prod = jnp.dot(x_ref[k], v_ref[k * size : (k + 1) * size, :], preferred_element_type=F32)
        add_chunk(k, prod, acc, o_ref)


def next_terms(x, v):
    rows, width = x.shape[1], v.shape[1]
    return call(
        next_kernel,
        jax.ShapeDtypeStruct((rows, width), BF16),
        (x, v),
        scratch=[pltpu.VMEM((rows, width), F32)],
        flops=2 * x.size * width,
    )


def fill(scratch, refs, pieces, lanes):
    row = 0
    for which, begin, rows in pieces:
        scratch[row : row + rows, :] = refs[which][begin : begin + rows, lanes]
        row += rows


def down_kernel(layout, info_ref, idx_ref, x_ref, own_ref, *refs):
    parts, (low_ref, sent_ref, up_ref, scratch) = refs[:-4], refs[-4:]
    rank, size, cols = low_ref.shape[0], x_ref.shape[2], own_ref.shape[1]
    up_ref[:rank, :] = own_ref[...]
    pieces = [p for pieces in layout[1:] for p in pieces]
    fill(up_ref.at[rank:], parts, pieces, slice(CHUNKS * size, CHUNKS * size + cols))
    low = jnp.zeros(low_ref.shape, F32)
    for first in range(0, len(layout), BATCH):
        group = layout[first : first + BATCH]
        prod = 0.0
        for k in range(CHUNKS):
            lanes = slice(k * size, (k + 1) * size)
            fill(scratch.at[k], parts, [p for pieces in group for p in pieces], lanes)
            prod += lax.dot_general(
                scratch[k, : len(group) * rank, :],
                x_ref[k],
                (((1,), (1,)), ((), ())),
                preferred_element_type=F32,
            )
        for k in range(len(group)):
            match = idx_ref[...] == info_ref[first + k]
            low = low + jnp.where(match, prod[k * rank : (k + 1) * rank, :], 0.0)
    low_ref[...] = low
    sent_ref[...] = low.astype(BF16)


def last_kernel(blocks, info_ref, idx_ref, low_ref, up_ref, *refs):
    terms, others, (out_ref, spread) = refs[:blocks], refs[blocks:-2], refs[-2:]
    rank = low_ref.shape[0]
    low = low_ref[...]
    for other in others:
        low = low + other[...].astype(F32)
    low = low.astype(BF16).astype(F32)
    adapters = up_ref.shape[0] // rank
    for k in range(adapters):
        match = idx_ref[...] == info_ref[k]
        spread[k * rank : (k + 1) * rank, :] = jnp.where(match, low, 0.0).astype(BF16)
    lora = lax.dot_general(
        spread[...], up_ref[...], (((0,), (0,)), ((), ())), preferred_element_type=F32
    )
    total = lora.astype(BF16).astype(F32)
    for n, term in enumerate(terms):
        total = total + jnp.where(info_ref[adapters + n] == 1, term[...].astype(F32), 0.0)
    out_ref[...] = total.astype(BF16)


def after(x, *others):
    return lax.optimization_barrier((x, *others))[0]


def build(mesh):
    groups, adapters = mesh.shape["groups"], mesh.shape["adapter"]
    tensors, replicas = mesh.shape["tensor"], mesh.shape["replica"]

    def shift(x, axis, by):
        size = mesh.shape[axis]
        return lax.ppermute(x, axis, [(i, (i + by) % size) for i in range(size)])

    def others(x, axis):
        return [shift(x, axis, by) for by in range(1, mesh.shape[axis])]

    def flip(x, bit):
        return lax.ppermute(x, "adapter", [(i, i ^ bit) for i in range(adapters)])

    def base_pairs(h, by):
        pairs = {}
        for ti in range(tensors):
            for ri in range(replicas):
                to = (ti + by) % tensors
                if to // per_half == (ri - h) % replicas:
                    pairs[ti * replicas + ri] = to * replicas + ri
        free = set(range(tensors * replicas)) - set(pairs.values())
        for source in range(tensors * replicas):
            if source not in pairs:
                chip = source // replicas
                near = [n for n in sorted(free) if n // replicas == chip] or sorted(free)
                pairs[source] = near[0]
                free.remove(near[0])
        return sorted(pairs.items())

    per_half = max(1, tensors // replicas)

    def shards(x, v, d, u, idx):
        g, a = lax.axis_index("groups"), lax.axis_index("adapter")
        t, r = lax.axis_index("tensor"), lax.axis_index("replica")
        tokens, rank, wide = x.shape[0], d.shape[2], d.shape[1]
        cols = u.shape[2]
        row = idx.reshape(1, tokens)

        held = [v] + others(v, "replica")

        down = d[0].T
        own = jnp.concatenate([down, u[0]], axis=1)
        share = rank // (groups * replicas)
        mine = lax.dynamic_slice_in_dim(own, (g * replicas + r) * share, share, 0)
        bits = [1 << n for n in reversed(range((adapters - 1).bit_length()))]
        pieces = {}
        direct = [(bit, flip(mine, bit)) for bit in bits]

        blocks, recvs = [], []

        def base(h):
            terms, cuts = first_terms(x, v) if h == 0 else (next_terms(xs, held[h]), None)
            half = lax.rem(r - h + replicas, replicas)
            begin = half * per_half

            def cut(n):
                if per_half == 1:
                    return terms
                at = jnp.clip(n - begin, 0, per_half - 1) * cols
                return lax.dynamic_slice_in_dim(terms, at, cols, 1)

            blocks.append(cut(t))
            for by in range(1, tensors):
                block = after(cut(lax.rem(t + by, tensors)), *[piece for _, piece in direct])
                recvs.append(lax.ppermute(block, ("tensor", "replica"), base_pairs(h, by)))
            return terms, cuts

        order = sorted(range(1, adapters), key=lambda p: (bin(p).count("1"), p))
        halves = [lax.rem(r - h + replicas, replicas) * per_half for h in range(replicas)]
        here = [((t >= n) & (t < n + per_half)).astype(jnp.int32) for n in halves]
        info = [a] + [lax.bitwise_xor(a, jnp.int32(p)) for p in order]
        info = jnp.stack(info + here + [f for f in here for _ in range(1, tensors)])
        xs = None
        x, info = lax.optimization_barrier((x, info, mine))[:2]
        done = []
        for h in range(replicas):
            terms, cuts = base(h)
            done.append(terms)
            xs = cuts if h == 0 else xs
        for bit, piece in direct:
            pieces[bit] = after(piece, done[0])
            for prior in [p for p in pieces if p > bit and not p & bit]:
                pieces[prior | bit] = flip(pieces[prior], bit)
        arrays, layout = [], [[(0, 0, rank)]]

        def keep(array):
            arrays.append(array)
            return len(arrays)

        for p in order:
            layout.append([])
            piece = pieces[p]
            for member in [piece] + others(piece, "groups"):
                for array in [member] + others(member, "replica"):
                    layout[-1].append((keep(array), 0, share))

        low, sent, every = call(
            functools.partial(down_kernel, layout),
            (jax.ShapeDtypeStruct((rank, tokens), F32), jax.ShapeDtypeStruct((rank, tokens), BF16),
                jax.ShapeDtypeStruct((adapters * rank, cols), BF16)),
            (info, row, after(xs, *recvs), u[0], down, *arrays),
            scratch=[
                pltpu.VMEM((CHUNKS, min(BATCH, adapters) * rank, wide // CHUNKS), BF16),
            ],
            flops=2 * x.size * rank * adapters,
            specs=[SMEM] + [VMEM] * (4 + len(arrays)),
        )
        lows = others(sent, "tensor")
        terms = blocks + recvs
        return call(
            functools.partial(last_kernel, len(terms)),
            jax.ShapeDtypeStruct((tokens, cols), BF16),
            (info, row, low, every, *terms, *lows),
            scratch=[pltpu.VMEM((adapters * rank, tokens), BF16)],
            flops=2 * tokens * rank * adapters * cols,
            specs=[SMEM] + [VMEM] * (3 + len(terms) + len(lows)),
        )

    return shards


def solution(mesh):
    return jax.shard_map(
        build(mesh),
        mesh=mesh,
        in_specs=(
            P(("groups", "adapter", "replica"), "tensor"),
            P("tensor", "replica"),
            P("adapter", "tensor", None),
            P("adapter", None, "tensor"),
            P(("groups", "adapter", "replica"), None),
        ),
        out_specs=P(("groups", "adapter", "replica"), "tensor"),
        check_vma=False,
    )
```

```python
import functools

import jax
import jax.numpy as jnp
from jax import lax
from jax.experimental import pallas as pl
from jax.experimental.pallas import tpu as pltpu
from jax.sharding import PartitionSpec as P

F32 = jnp.float32
BF16 = jnp.bfloat16
VMEM = pl.BlockSpec(memory_space=pltpu.VMEM)
SMEM = pl.BlockSpec(memory_space=pltpu.SMEM)
HBM = pl.BlockSpec(memory_space=pltpu.HBM)
CHUNKS = 4
BATCH = 4


def call(kernel, outs, args, scratch=(), flops=0, limit=16, specs=None):
    size = sum(a.size * a.dtype.itemsize for a in args)
    return pl.pallas_call(
        kernel,
        out_shape=outs,
        in_specs=specs or [VMEM] * len(args),
        out_specs=jax.tree.map(lambda _: VMEM, outs),
        scratch_shapes=scratch,
        compiler_params=pltpu.CompilerParams(vmem_limit_bytes=limit << 20),
        cost_estimate=pl.CostEstimate(flops=flops, bytes_accessed=size, transcendentals=0),
    )(*args)


def chunks(refs, buffers, sems):
    copies = []
    for k in range(CHUNKS):
        copies.append([])
        for n, (ref, buffer) in enumerate(zip(refs, buffers)):
            copy = pltpu.make_async_copy(ref(k), buffer.at[k], sems.at[n, k])
            copy.start()
            copies[-1].append(copy)
    return copies


def part(ref, axis):
    size = ref.shape[axis] // CHUNKS
    if axis == 0:
        return lambda k: ref.at[pl.ds(k * size, size)]
    return lambda k: ref.at[:, pl.ds(k * size, size)]


def share_kernel(info_ref, down_ref, up_ref, out_ref, sems):
    share, wide = out_ref.shape[0], down_ref.shape[1]
    rows = pl.ds(pl.multiple_of(info_ref[0] * share, share), share)
    copies = [
        pltpu.make_async_copy(down_ref.at[rows], out_ref.at[:, :wide], sems.at[0]),
        pltpu.make_async_copy(up_ref.at[rows], out_ref.at[:, wide:], sems.at[1]),
    ]
    for copy in copies:
        copy.start()
    for copy in copies:
        copy.wait()


def add_chunk(k, prod, acc, out_ref):
    if k > 0:
        prod = prod + acc[...]
    if k < CHUNKS - 1:
        acc[...] = prod
    else:
        out_ref[...] = prod.astype(BF16)


def first_kernel(x_ref, v_ref, o_ref, x_out, v_buf, acc, sems):
    copies = chunks((part(x_ref, 1), part(v_ref, 0)), (x_out, v_buf), sems)
    for k in range(CHUNKS):
        for copy in copies[k]:
            copy.wait()
        add_chunk(k, jnp.dot(x_out[k], v_buf[k], preferred_element_type=F32), acc, o_ref)


def first_terms(x, v):
    rows, wide, width = x.shape[0], x.shape[1], v.shape[1]
    cut = (CHUNKS, rows, wide // CHUNKS)
    return call(
        first_kernel,
        (jax.ShapeDtypeStruct((rows, width), BF16), jax.ShapeDtypeStruct(cut, BF16)),
        (x, v),
        scratch=[
            pltpu.VMEM((CHUNKS, wide // CHUNKS, width), BF16),
            pltpu.VMEM((rows, width), F32),
            pltpu.SemaphoreType.DMA((2, CHUNKS)),
        ],
        flops=2 * x.size * width,
        limit=48,
        specs=[HBM] * 2,
    )


def next_kernel(x_ref, v_ref, o_ref, v_buf, acc, sems):
    copies = chunks((part(v_ref, 0),), (v_buf,), sems)
    for k in range(CHUNKS):
        copies[k][0].wait()
        add_chunk(k, jnp.dot(x_ref[k], v_buf[k], preferred_element_type=F32), acc, o_ref)


def next_terms(x, v):
    rows, wide, width = x.shape[1], v.shape[0], v.shape[1]
    return call(
        next_kernel,
        jax.ShapeDtypeStruct((rows, width), BF16),
        (x, v),
        scratch=[
            pltpu.VMEM((CHUNKS, wide // CHUNKS, width), BF16),
            pltpu.VMEM((rows, width), F32),
            pltpu.SemaphoreType.DMA((1, CHUNKS)),
        ],
        flops=2 * x.size * width,
        limit=48,
        specs=[VMEM, HBM],
    )


def fill(scratch, refs, pieces, lanes):
    row = 0
    for which, begin, rows in pieces:
        scratch[row : row + rows, :] = refs[which][begin : begin + rows, lanes]
        row += rows


def down_kernel(layout, info_ref, idx_ref, x_ref, own_ref, *refs):
    parts, (low_ref, sent_ref, up_ref, scratch) = refs[:-4], refs[-4:]
    rank, size, cols = low_ref.shape[0], x_ref.shape[2], own_ref.shape[1]
    up_ref[:rank, :] = own_ref[...]
    pieces = [p for pieces in layout[1:] for p in pieces]
    fill(up_ref.at[rank:], parts, pieces, slice(CHUNKS * size, CHUNKS * size + cols))
    low = jnp.zeros(low_ref.shape, F32)
    for first in range(0, len(layout), BATCH):
        group = layout[first : first + BATCH]
        prod = 0.0
        for k in range(CHUNKS):
            lanes = slice(k * size, (k + 1) * size)
            fill(scratch.at[k], parts, [p for pieces in group for p in pieces], lanes)
            prod += lax.dot_general(
                scratch[k, : len(group) * rank, :],
                x_ref[k],
                (((1,), (1,)), ((), ())),
                preferred_element_type=F32,
            )
        for k in range(len(group)):
            match = idx_ref[...] == info_ref[1 + first + k]
            low = low + jnp.where(match, prod[k * rank : (k + 1) * rank, :], 0.0)
    low_ref[...] = low
    sent_ref[...] = low.astype(BF16)


def sum_kernel(adapters, info_ref, *refs):
    terms, out_ref = refs[:-1], refs[-1]
    total = jnp.zeros(out_ref.shape, F32)
    for n, term in enumerate(terms):
        total = total + jnp.where(info_ref[1 + adapters + n] == 1, term[...].astype(F32), 0.0)
    out_ref[...] = total


def last_kernel(info_ref, idx_ref, base_ref, up_ref, low_ref, *refs):
    others, (out_ref, spread) = refs[:-2], refs[-2:]
    rank = low_ref.shape[0]
    low = low_ref[...]
    for other in others:
        low = low + other[...].astype(F32)
    low = low.astype(BF16).astype(F32)
    for k in range(up_ref.shape[0] // rank):
        match = idx_ref[...] == info_ref[1 + k]
        spread[k * rank : (k + 1) * rank, :] = jnp.where(match, low, 0.0).astype(BF16)
    lora = lax.dot_general(
        spread[...], up_ref[...], (((0,), (0,)), ((), ())), preferred_element_type=F32
    )
    out_ref[...] = (base_ref[...] + lora.astype(BF16).astype(F32)).astype(BF16)


def after(x, *others):
    return lax.optimization_barrier((x, *others))[0]


def build(mesh):
    groups, adapters = mesh.shape["groups"], mesh.shape["adapter"]
    tensors, replicas = mesh.shape["tensor"], mesh.shape["replica"]

    def shift(x, axis, by):
        size = mesh.shape[axis]
        return lax.ppermute(x, axis, [(i, (i + by) % size) for i in range(size)])

    def others(x, axis):
        return [shift(x, axis, by) for by in range(1, mesh.shape[axis])]

    def base_pairs(h, by):
        pairs = {}
        for ti in range(tensors):
            for ri in range(replicas):
                to = (ti + by) % tensors
                if to // per_half == (ri - h) % replicas:
                    pairs[ti * replicas + ri] = to * replicas + ri
        free = set(range(tensors * replicas)) - set(pairs.values())
        for source in range(tensors * replicas):
            if source not in pairs:
                chip = source // replicas
                near = [n for n in sorted(free) if n // replicas == chip] or sorted(free)
                pairs[source] = near[0]
                free.remove(near[0])
        return sorted(pairs.items())

    per_half = max(1, tensors // replicas)

    def shards(x, v, d, u, idx):
        g, a = lax.axis_index("groups"), lax.axis_index("adapter")
        t, r = lax.axis_index("tensor"), lax.axis_index("replica")
        tokens, rank, wide = x.shape[0], d.shape[2], d.shape[1]
        cols = u.shape[2]
        row = idx.reshape(1, tokens)

        order = [n * sign for n in range(1, adapters // 2 + 1) for sign in (1, -1)][: adapters - 1]
        halves = [lax.rem(r - h + replicas, replicas) * per_half for h in range(replicas)]
        here = [((t >= n) & (t < n + per_half)).astype(jnp.int32) for n in halves]
        info = [g * replicas + r, a] + [lax.rem(a - p + adapters, adapters) for p in order]
        info = jnp.stack(info + here + [f for f in here for _ in range(1, tensors)])

        held = [v] + others(v, "replica")

        down = d[0].T
        share = rank // (groups * replicas)
        mine = call(
            share_kernel,
            jax.ShapeDtypeStruct((share, wide + cols), BF16),
            (info, down, u[0]),
            scratch=[pltpu.SemaphoreType.DMA((2,))],
            limit=61,
            specs=[SMEM, HBM, HBM],
        )
        pieces = {1: shift(mine, "adapter", 1)} if adapters > 1 else {}

        blocks, recvs = [], []

        def base(h, gate):
            terms, cuts = first_terms(x, v) if h == 0 else (next_terms(xs, held[h]), None)
            half = lax.rem(r - h + replicas, replicas)
            begin = half * per_half

            def cut(n):
                if per_half == 1:
                    return terms
                at = jnp.clip(n - begin, 0, per_half - 1) * cols
                return lax.dynamic_slice_in_dim(terms, at, cols, 1)

            blocks.append(cut(t))
            for by in range(1, tensors):
                block = after(cut(lax.rem(t + by, tensors)), *gate)
                recvs.append(lax.ppermute(block, ("tensor", "replica"), base_pairs(h, by)))
            return terms, cuts

        xs = None
        x = after(x, mine)
        first, xs = base(0, [])
        for p in order[1:]:
            sign = 1 if p > 0 else -1
            behind = after(mine, first) if p == -1 else pieces[p - sign]
            pieces[p] = shift(behind, "adapter", sign)
        for h in range(1, replicas):
            base(h, [])
        arrays, layout = [], [[(0, 0, rank)]]

        def keep(array):
            arrays.append(array)
            return len(arrays)

        for p in order:
            layout.append([])
            piece = pieces[p]
            for member in [piece] + others(piece, "groups"):
                for array in [member] + others(member, "replica"):
                    layout[-1].append((keep(array), 0, share))

        low, sent, every = call(
            functools.partial(down_kernel, layout),
            (jax.ShapeDtypeStruct((rank, tokens), F32), jax.ShapeDtypeStruct((rank, tokens), BF16),
                jax.ShapeDtypeStruct((adapters * rank, cols), BF16)),
            (info, row, after(xs, *recvs[: tensors - 1]), u[0], down, *arrays),
            scratch=[
                pltpu.VMEM((CHUNKS, min(BATCH, adapters) * rank, wide // CHUNKS), BF16),
            ],
            flops=2 * x.size * rank * adapters,
            specs=[SMEM] + [VMEM] * (4 + len(arrays)),
        )
        lows = others(sent, "tensor")
        terms = blocks + recvs
        total = call(
            functools.partial(sum_kernel, adapters),
            jax.ShapeDtypeStruct((tokens, cols), F32),
            (info, *terms),
            flops=len(terms) * tokens * cols,
            specs=[SMEM] + [VMEM] * len(terms),
        )
        return call(
            last_kernel,
            jax.ShapeDtypeStruct((tokens, cols), BF16),
            (info, row, total, every, low, *lows),
            scratch=[pltpu.VMEM((adapters * rank, tokens), BF16)],
            flops=2 * tokens * rank * adapters * cols,
            specs=[SMEM] + [VMEM] * (4 + len(lows)),
        )

    return shards


def solution(mesh):
    return jax.shard_map(
        build(mesh),
        mesh=mesh,
        in_specs=(
            P(("groups", "adapter", "replica"), "tensor"),
            P("tensor", "replica"),
            P("adapter", "tensor", None),
            P("adapter", None, "tensor"),
            P(("groups", "adapter", "replica"), None),
        ),
        out_specs=P(("groups", "adapter", "replica"), "tensor"),
        check_vma=False,
    )
```

```python
import functools

import jax
import jax.numpy as jnp
from jax import lax
from jax.experimental import pallas as pl
from jax.experimental.pallas import tpu as pltpu
from jax.sharding import PartitionSpec as P

F32 = jnp.float32
BF16 = jnp.bfloat16
VMEM = pl.BlockSpec(memory_space=pltpu.VMEM)
SMEM = pl.BlockSpec(memory_space=pltpu.SMEM)
HBM = pl.BlockSpec(memory_space=pltpu.HBM)
CHUNKS = 4
BATCH = 4


def call(kernel, outs, args, scratch=(), flops=0, limit=16, specs=None):
    size = sum(a.size * a.dtype.itemsize for a in args)
    return pl.pallas_call(
        kernel,
        out_shape=outs,
        in_specs=specs or [VMEM] * len(args),
        out_specs=jax.tree.map(lambda _: VMEM, outs),
        scratch_shapes=scratch,
        compiler_params=pltpu.CompilerParams(vmem_limit_bytes=limit << 20),
        cost_estimate=pl.CostEstimate(flops=flops, bytes_accessed=size, transcendentals=0),
    )(*args)


def chunks(refs, buffers, sems):
    copies = []
    for k in range(CHUNKS):
        copies.append([])
        for n, (ref, buffer) in enumerate(zip(refs, buffers)):
            copy = pltpu.make_async_copy(ref(k), buffer.at[k], sems.at[n, k])
            copy.start()
            copies[-1].append(copy)
    return copies


def part(ref, axis):
    size = ref.shape[axis] // CHUNKS
    if axis == 0:
        return lambda k: ref.at[pl.ds(k * size, size)]
    return lambda k: ref.at[:, pl.ds(k * size, size)]


def pack_kernel(*refs):
    row = 0
    for ref in refs[:-1]:
        refs[-1][row : row + ref.shape[0], :] = ref[...]
        row += ref.shape[0]


def add_chunk(k, prod, acc, out_ref):
    if k > 0:
        prod = prod + acc[...]
    if k < CHUNKS - 1:
        acc[...] = prod
    else:
        out_ref[...] = prod.astype(BF16)


def first_kernel(x_ref, v_ref, o_ref, x_out, v_buf, acc, sems):
    copies = chunks((part(x_ref, 1), part(v_ref, 0)), (x_out, v_buf), sems)
    for k in range(CHUNKS):
        for copy in copies[k]:
            copy.wait()
        add_chunk(k, jnp.dot(x_out[k], v_buf[k], preferred_element_type=F32), acc, o_ref)


def first_terms(x, v):
    rows, wide, width = x.shape[0], x.shape[1], v.shape[1]
    cut = (CHUNKS, rows, wide // CHUNKS)
    return call(
        first_kernel,
        (jax.ShapeDtypeStruct((rows, width), BF16), jax.ShapeDtypeStruct(cut, BF16)),
        (x, v),
        scratch=[
            pltpu.VMEM((CHUNKS, wide // CHUNKS, width), BF16),
            pltpu.VMEM((rows, width), F32),
            pltpu.SemaphoreType.DMA((2, CHUNKS)),
        ],
        flops=2 * x.size * width,
        limit=48,
        specs=[HBM] * 2,
    )


def next_kernel(x_ref, v_ref, o_ref, v_buf, acc, sems):
    copies = chunks((part(v_ref, 0),), (v_buf,), sems)
    for k in range(CHUNKS):
        copies[k][0].wait()
        add_chunk(k, jnp.dot(x_ref[k], v_buf[k], preferred_element_type=F32), acc, o_ref)


def next_terms(x, v):
    rows, wide, width = x.shape[1], v.shape[0], v.shape[1]
    return call(
        next_kernel,
        jax.ShapeDtypeStruct((rows, width), BF16),
        (x, v),
        scratch=[
            pltpu.VMEM((CHUNKS, wide // CHUNKS, width), BF16),
            pltpu.VMEM((rows, width), F32),
            pltpu.SemaphoreType.DMA((1, CHUNKS)),
        ],
        flops=2 * x.size * width,
        limit=48,
        specs=[VMEM, HBM],
    )


def fill(scratch, refs, pieces, lanes):
    row = 0
    for which, begin, rows in pieces:
        scratch[row : row + rows, :] = refs[which][begin : begin + rows, lanes]
        row += rows


def down_kernel(layout, info_ref, idx_ref, x_ref, own_ref, *refs):
    parts, (low_ref, sent_ref, up_ref, scratch) = refs[:-4], refs[-4:]
    rank, size, cols = low_ref.shape[0], x_ref.shape[2], own_ref.shape[1]
    up_ref[:rank, :] = own_ref[...]
    pieces = [p for pieces in layout[1:] for p in pieces]
    fill(up_ref.at[rank:], parts, pieces, slice(CHUNKS * size, CHUNKS * size + cols))
    low = jnp.zeros(low_ref.shape, F32)
    for first in range(0, len(layout), BATCH):
        group = layout[first : first + BATCH]
        prod = 0.0
        for k in range(CHUNKS):
            lanes = slice(k * size, (k + 1) * size)
            fill(scratch.at[k], parts, [p for pieces in group for p in pieces], lanes)
            prod += lax.dot_general(
                scratch[k, : len(group) * rank, :],
                x_ref[k],
                (((1,), (1,)), ((), ())),
                preferred_element_type=F32,
            )
        for k in range(len(group)):
            match = idx_ref[...] == info_ref[first + k]
            low = low + jnp.where(match, prod[k * rank : (k + 1) * rank, :], 0.0)
    low_ref[...] = low
    sent_ref[...] = low.astype(BF16)


def sum_kernel(adapters, info_ref, *refs):
    terms, out_ref = refs[:-1], refs[-1]
    total = jnp.zeros(out_ref.shape, F32)
    for n, term in enumerate(terms):
        total = total + jnp.where(info_ref[adapters + n] == 1, term[...].astype(F32), 0.0)
    out_ref[...] = total


def last_kernel(info_ref, idx_ref, base_ref, up_ref, low_ref, *refs):
    others, (out_ref, spread) = refs[:-2], refs[-2:]
    rank = low_ref.shape[0]
    low = low_ref[...]
    for other in others:
        low = low + other[...].astype(F32)
    low = low.astype(BF16).astype(F32)
    for k in range(up_ref.shape[0] // rank):
        match = idx_ref[...] == info_ref[k]
        spread[k * rank : (k + 1) * rank, :] = jnp.where(match, low, 0.0).astype(BF16)
    lora = lax.dot_general(
        spread[...], up_ref[...], (((0,), (0,)), ((), ())), preferred_element_type=F32
    )
    out_ref[...] = (base_ref[...] + lora.astype(BF16).astype(F32)).astype(BF16)


def after(x, *others):
    return lax.optimization_barrier((x, *others))[0]


def build(mesh):
    groups, adapters = mesh.shape["groups"], mesh.shape["adapter"]
    tensors, replicas = mesh.shape["tensor"], mesh.shape["replica"]

    def shift(x, axis, by):
        size = mesh.shape[axis]
        return lax.ppermute(x, axis, [(i, (i + by) % size) for i in range(size)])

    def others(x, axis):
        return [shift(x, axis, by) for by in range(1, mesh.shape[axis])]

    def base_pairs(h, by):
        pairs = {}
        for ti in range(tensors):
            for ri in range(replicas):
                to = (ti + by) % tensors
                if to // per_half == (ri - h) % replicas:
                    pairs[ti * replicas + ri] = to * replicas + ri
        free = set(range(tensors * replicas)) - set(pairs.values())
        for source in range(tensors * replicas):
            if source not in pairs:
                chip = source // replicas
                near = [n for n in sorted(free) if n // replicas == chip] or sorted(free)
                pairs[source] = near[0]
                free.remove(near[0])
        return sorted(pairs.items())

    per_half = max(1, tensors // replicas)

    def shards(x, v, d, u, idx):
        g, a = lax.axis_index("groups"), lax.axis_index("adapter")
        t, r = lax.axis_index("tensor"), lax.axis_index("replica")
        tokens, rank, wide = x.shape[0], d.shape[2], d.shape[1]
        cols = u.shape[2]
        row = idx.reshape(1, tokens)

        order = [n * sign for n in range(1, adapters // 2 + 1) for sign in (1, -1)][: adapters - 1]
        halves = [lax.rem(r - h + replicas, replicas) * per_half for h in range(replicas)]
        here = [((t >= n) & (t < n + per_half)).astype(jnp.int32) for n in halves]
        info = [a] + [lax.rem(a - p + adapters, adapters) for p in order]
        info = jnp.stack(info + here + [f for f in here for _ in range(1, tensors)])

        held = [v] + others(v, "replica")

        down = d[0].T
        share = rank // (groups * replicas)
        own = jnp.concatenate([down, u[0]], axis=1)
        mine = lax.dynamic_slice_in_dim(own, (g * replicas + r) * share, share, 0)
        pieces = {1: shift(mine, "adapter", 1)} if adapters > 1 else {}

        blocks, recvs = [], []

        def base(h, gate):
            terms, cuts = first_terms(x, v) if h == 0 else (next_terms(xs, held[h]), None)
            half = lax.rem(r - h + replicas, replicas)
            begin = half * per_half

            def cut(n):
                if per_half == 1:
                    return terms
                at = jnp.clip(n - begin, 0, per_half - 1) * cols
                return lax.dynamic_slice_in_dim(terms, at, cols, 1)

            blocks.append(cut(t))
            for by in range(1, tensors):
                block = after(cut(lax.rem(t + by, tensors)), *gate)
                recvs.append(lax.ppermute(block, ("tensor", "replica"), base_pairs(h, by)))
            return terms, cuts

        xs = None
        x, info = lax.optimization_barrier((x, info, mine))[:2]
        near = [p for p in order if abs(p) == 1]
        for p in near[1:]:
            pieces[p] = shift(mine, "adapter", p)
        first, xs = base(0, [pieces[n] for n in near])
        for p, piece in zip(near, lax.optimization_barrier((*[pieces[p] for p in near], first))):
            pieces[p] = piece
        for p in order[len(near) :]:
            sign = 1 if p > 0 else -1
            pieces[p] = shift(pieces[p - sign], "adapter", sign)
        for h in range(1, replicas):
            base(h, [pieces[order[-1]]])
        arrays, layout = [down], [[(0, 0, rank)]] + [[] for _ in order]

        def keep(k, array, begin=0):
            where = [n for n, other in enumerate(arrays) if other is array]
            if not where:
                arrays.append(array)
            layout[k].append((where[0] if where else len(arrays) - 1, begin, share))

        shares = [
            (1 + n, member)
            for n, p in enumerate(order)
            for member in [pieces[p]] + others(pieces[p], "groups")
        ]
        for k, member in shares:
            keep(k, member)
        if replicas > 1:
            (last, member), bundles = shares[-1], [shares[n : n + 2] for n in range(0, len(shares) - 1, 2)]
            bundles[-1] = [s for s in bundles[-1] if s is not shares[-1]]
            held_back = blocks
            for bundle in bundles:
                members = lax.optimization_barrier((*[array for _, array in bundle], *held_back))[: len(bundle)]
                packed = members[0]
                if len(bundle) > 1:
                    shape = (share * len(bundle), wide + cols)
                    packed = call(pack_kernel, jax.ShapeDtypeStruct(shape, BF16), tuple(members))
                for other in others(packed, "replica"):
                    for n, (k, _) in enumerate(bundle):
                        keep(k, other, n * share)
            for other in others(member, "replica"):
                keep(last, other)

        low, sent, every = call(
            functools.partial(down_kernel, layout),
            (jax.ShapeDtypeStruct((rank, tokens), F32), jax.ShapeDtypeStruct((rank, tokens), BF16),
                jax.ShapeDtypeStruct((adapters * rank, cols), BF16)),
            (info, row, after(xs, *recvs[: tensors - 1]), u[0], *arrays),
            scratch=[
                pltpu.VMEM((CHUNKS, min(BATCH, adapters) * rank, wide // CHUNKS), BF16),
            ],
            flops=2 * x.size * rank * adapters,
            specs=[SMEM] + [VMEM] * (3 + len(arrays)),
        )
        lows = others(sent, "tensor")
        terms = blocks + recvs
        total = call(
            functools.partial(sum_kernel, adapters),
            jax.ShapeDtypeStruct((tokens, cols), F32),
            (info, *terms),
            flops=len(terms) * tokens * cols,
            specs=[SMEM] + [VMEM] * len(terms),
        )
        return call(
            last_kernel,
            jax.ShapeDtypeStruct((tokens, cols), BF16),
            (info, row, total, every, low, *lows),
            scratch=[pltpu.VMEM((adapters * rank, tokens), BF16)],
            flops=2 * tokens * rank * adapters * cols,
            specs=[SMEM] + [VMEM] * (4 + len(lows)),
        )

    return shards


def solution(mesh):
    return jax.shard_map(
        build(mesh),
        mesh=mesh,
        in_specs=(
            P(("groups", "adapter", "replica"), "tensor"),
            P("tensor", "replica"),
            P("adapter", "tensor", None),
            P("adapter", None, "tensor"),
            P(("groups", "adapter", "replica"), None),
        ),
        out_specs=P(("groups", "adapter", "replica"), "tensor"),
        check_vma=False,
    )
```

```python
import functools

import jax
import jax.numpy as jnp
from jax import lax
from jax.experimental import pallas as pl
from jax.experimental.pallas import tpu as pltpu
from jax.sharding import PartitionSpec as P

F32 = jnp.float32
BF16 = jnp.bfloat16
VMEM = pl.BlockSpec(memory_space=pltpu.VMEM)
SMEM = pl.BlockSpec(memory_space=pltpu.SMEM)
HBM = pl.BlockSpec(memory_space=pltpu.HBM)
CHUNKS = 4
BATCH = 4


def call(kernel, outs, args, scratch=(), flops=0, limit=16, specs=None):
    size = sum(a.size * a.dtype.itemsize for a in args)
    return pl.pallas_call(
        kernel,
        out_shape=outs,
        in_specs=specs or [VMEM] * len(args),
        out_specs=jax.tree.map(lambda _: VMEM, outs),
        scratch_shapes=scratch,
        compiler_params=pltpu.CompilerParams(vmem_limit_bytes=limit << 20),
        cost_estimate=pl.CostEstimate(flops=flops, bytes_accessed=size, transcendentals=0),
    )(*args)


def chunks(refs, buffers, sems):
    copies = []
    for k in range(CHUNKS):
        copies.append([])
        for n, (ref, buffer) in enumerate(zip(refs, buffers)):
            copy = pltpu.make_async_copy(ref(k), buffer.at[k], sems.at[n, k])
            copy.start()
            copies[-1].append(copy)
    return copies


def part(ref, axis):
    size = ref.shape[axis] // CHUNKS
    if axis == 0:
        return lambda k: ref.at[pl.ds(k * size, size)]
    return lambda k: ref.at[:, pl.ds(k * size, size)]


def pack_kernel(*refs):
    row = 0
    for ref in refs[:-1]:
        refs[-1][row : row + ref.shape[0], :] = ref[...]
        row += ref.shape[0]


def add_chunk(k, prod, acc, out_ref):
    if k > 0:
        prod = prod + acc[...]
    if k < CHUNKS - 1:
        acc[...] = prod
    else:
        out_ref[...] = prod.astype(BF16)


def first_kernel(x_ref, v_ref, o_ref, x_out, v_buf, acc, sems):
    copies = chunks((part(x_ref, 1), part(v_ref, 0)), (x_out, v_buf), sems)
    for k in range(CHUNKS):
        for copy in copies[k]:
            copy.wait()
        add_chunk(k, jnp.dot(x_out[k], v_buf[k], preferred_element_type=F32), acc, o_ref)


def first_terms(x, v):
    rows, wide, width = x.shape[0], x.shape[1], v.shape[1]
    cut = (CHUNKS, rows, wide // CHUNKS)
    return call(
        first_kernel,
        (jax.ShapeDtypeStruct((rows, width), BF16), jax.ShapeDtypeStruct(cut, BF16)),
        (x, v),
        scratch=[
            pltpu.VMEM((CHUNKS, wide // CHUNKS, width), BF16),
            pltpu.VMEM((rows, width), F32),
            pltpu.SemaphoreType.DMA((2, CHUNKS)),
        ],
        flops=2 * x.size * width,
        limit=48,
        specs=[HBM] * 2,
    )


def next_kernel(x_ref, v_ref, o_ref, v_buf, acc, sems):
    copies = chunks((part(v_ref, 0),), (v_buf,), sems)
    for k in range(CHUNKS):
        copies[k][0].wait()
        add_chunk(k, jnp.dot(x_ref[k], v_buf[k], preferred_element_type=F32), acc, o_ref)


def next_terms(x, v):
    rows, wide, width = x.shape[1], v.shape[0], v.shape[1]
    return call(
        next_kernel,
        jax.ShapeDtypeStruct((rows, width), BF16),
        (x, v),
        scratch=[
            pltpu.VMEM((CHUNKS, wide // CHUNKS, width), BF16),
            pltpu.VMEM((rows, width), F32),
            pltpu.SemaphoreType.DMA((1, CHUNKS)),
        ],
        flops=2 * x.size * width,
        limit=48,
        specs=[VMEM, HBM],
    )


def fill(scratch, refs, pieces, lanes):
    row = 0
    for which, begin, rows in pieces:
        scratch[row : row + rows, :] = refs[which][begin : begin + rows, lanes]
        row += rows


def down_kernel(layout, info_ref, idx_ref, x_ref, own_ref, *refs):
    parts, (low_ref, sent_ref, up_ref, scratch) = refs[:-4], refs[-4:]
    rank, size, cols = low_ref.shape[0], x_ref.shape[2], own_ref.shape[1]
    up_ref[:rank, :] = own_ref[...]
    pieces = [p for pieces in layout[1:] for p in pieces]
    fill(up_ref.at[rank:], parts, pieces, slice(CHUNKS * size, CHUNKS * size + cols))
    low = jnp.zeros(low_ref.shape, F32)
    for first in range(0, len(layout), BATCH):
        group = layout[first : first + BATCH]
        prod = 0.0
        for k in range(CHUNKS):
            lanes = slice(k * size, (k + 1) * size)
            fill(scratch.at[k], parts, [p for pieces in group for p in pieces], lanes)
            prod += lax.dot_general(
                scratch[k, : len(group) * rank, :],
                x_ref[k],
                (((1,), (1,)), ((), ())),
                preferred_element_type=F32,
            )
        for k in range(len(group)):
            match = idx_ref[...] == info_ref[first + k]
            low = low + jnp.where(match, prod[k * rank : (k + 1) * rank, :], 0.0)
    low_ref[...] = low
    sent_ref[...] = low.astype(BF16)


def sum_kernel(adapters, info_ref, *refs):
    terms, out_ref = refs[:-1], refs[-1]
    total = jnp.zeros(out_ref.shape, F32)
    for n, term in enumerate(terms):
        total = total + jnp.where(info_ref[adapters + n] == 1, term[...].astype(F32), 0.0)
    out_ref[...] = total


def last_kernel(info_ref, idx_ref, base_ref, up_ref, low_ref, *refs):
    others, (out_ref, spread) = refs[:-2], refs[-2:]
    rank = low_ref.shape[0]
    low = low_ref[...]
    for other in others:
        low = low + other[...].astype(F32)
    low = low.astype(BF16).astype(F32)
    for k in range(up_ref.shape[0] // rank):
        match = idx_ref[...] == info_ref[k]
        spread[k * rank : (k + 1) * rank, :] = jnp.where(match, low, 0.0).astype(BF16)
    lora = lax.dot_general(
        spread[...], up_ref[...], (((0,), (0,)), ((), ())), preferred_element_type=F32
    )
    out_ref[...] = (base_ref[...] + lora.astype(BF16).astype(F32)).astype(BF16)


def after(x, *others):
    return lax.optimization_barrier((x, *others))[0]


def build(mesh):
    groups, adapters = mesh.shape["groups"], mesh.shape["adapter"]
    tensors, replicas = mesh.shape["tensor"], mesh.shape["replica"]

    def shift(x, axis, by):
        size = mesh.shape[axis]
        return lax.ppermute(x, axis, [(i, (i + by) % size) for i in range(size)])

    def others(x, axis):
        return [shift(x, axis, by) for by in range(1, mesh.shape[axis])]

    def base_pairs(h, by):
        pairs = {}
        for ti in range(tensors):
            for ri in range(replicas):
                to = (ti + by) % tensors
                if to // per_half == (ri - h) % replicas:
                    pairs[ti * replicas + ri] = to * replicas + ri
        free = set(range(tensors * replicas)) - set(pairs.values())
        for source in range(tensors * replicas):
            if source not in pairs:
                chip = source // replicas
                near = [n for n in sorted(free) if n // replicas == chip] or sorted(free)
                pairs[source] = near[0]
                free.remove(near[0])
        return sorted(pairs.items())

    per_half = max(1, tensors // replicas)

    def shards(x, v, d, u, idx):
        g, a = lax.axis_index("groups"), lax.axis_index("adapter")
        t, r = lax.axis_index("tensor"), lax.axis_index("replica")
        tokens, rank, wide = x.shape[0], d.shape[2], d.shape[1]
        cols = u.shape[2]
        row = idx.reshape(1, tokens)

        order = [n * sign for n in range(1, adapters // 2 + 1) for sign in (1, -1)][: adapters - 1]
        halves = [lax.rem(r - h + replicas, replicas) * per_half for h in range(replicas)]
        here = [((t >= n) & (t < n + per_half)).astype(jnp.int32) for n in halves]
        info = [a] + [lax.rem(a - p + adapters, adapters) for p in order]
        info = jnp.stack(info + here + [f for f in here for _ in range(1, tensors)])

        held = [v] + others(v, "replica")

        down = d[0].T
        share = rank // (groups * replicas)
        own = jnp.concatenate([down, u[0]], axis=1)
        mine = lax.dynamic_slice_in_dim(own, (g * replicas + r) * share, share, 0)
        pieces = {1: shift(mine, "adapter", 1)} if adapters > 1 else {}

        blocks, recvs = [], []

        def base(h, gate):
            terms, cuts = first_terms(x, v) if h == 0 else (next_terms(xs, held[h]), None)
            half = lax.rem(r - h + replicas, replicas)
            begin = half * per_half

            def cut(n):
                if per_half == 1:
                    return terms
                at = jnp.clip(n - begin, 0, per_half - 1) * cols
                return lax.dynamic_slice_in_dim(terms, at, cols, 1)

            blocks.append(cut(t))
            for by in range(1, tensors):
                block = after(cut(lax.rem(t + by, tensors)), *gate)
                recvs.append(lax.ppermute(block, ("tensor", "replica"), base_pairs(h, by)))
            return terms, cuts

        xs = None
        x, info = lax.optimization_barrier((x, info, mine))[:2]
        near = [p for p in order if abs(p) == 1]
        for p in near[1:]:
            pieces[p] = shift(mine, "adapter", p)
        first, xs = base(0, [])
        for p, piece in zip(near, lax.optimization_barrier((*[pieces[p] for p in near], first))):
            pieces[p] = piece
        for p in order[len(near) :]:
            sign = 1 if p > 0 else -1
            pieces[p] = shift(pieces[p - sign], "adapter", sign)
        for h in range(1, replicas):
            base(h, [pieces[order[-1]]])

        arrays, layout = [down], [[(0, 0, rank)]] + [[] for _ in order]

        def keep(array, pair):
            arrays.append(array)
            for n, p in enumerate(pair):
                layout[1 + order.index(p)].append((len(arrays) - 1, n * share, share))

        for n in range(0, len(order), 2):
            pair = order[n : n + 2]
            packed = pieces[pair[0]]
            if len(pair) > 1:
                packed = call(
                    pack_kernel,
                    jax.ShapeDtypeStruct((share * len(pair), wide + cols), BF16),
                    tuple(pieces[p] for p in pair),
                )
            for member in [packed] + others(packed, "groups"):
                keep(member, pair)
                for other in others(member, "replica"):
                    keep(other, pair)

        low, sent, every = call(
            functools.partial(down_kernel, layout),
            (jax.ShapeDtypeStruct((rank, tokens), F32), jax.ShapeDtypeStruct((rank, tokens), BF16),
                jax.ShapeDtypeStruct((adapters * rank, cols), BF16)),
            (info, row, after(xs, *recvs[: tensors - 1]), u[0], *arrays),
            scratch=[
                pltpu.VMEM((CHUNKS, min(BATCH, adapters) * rank, wide // CHUNKS), BF16),
            ],
            flops=2 * x.size * rank * adapters,
            specs=[SMEM] + [VMEM] * (3 + len(arrays)),
        )
        lows = others(sent, "tensor")
        terms = blocks + recvs
        total = call(
            functools.partial(sum_kernel, adapters),
            jax.ShapeDtypeStruct((tokens, cols), F32),
            (info, *terms),
            flops=len(terms) * tokens * cols,
            specs=[SMEM] + [VMEM] * len(terms),
        )
        return call(
            last_kernel,
            jax.ShapeDtypeStruct((tokens, cols), BF16),
            (info, row, total, every, low, *lows),
            scratch=[pltpu.VMEM((adapters * rank, tokens), BF16)],
            flops=2 * tokens * rank * adapters * cols,
            specs=[SMEM] + [VMEM] * (4 + len(lows)),
        )

    return shards


def solution(mesh):
    return jax.shard_map(
        build(mesh),
        mesh=mesh,
        in_specs=(
            P(("groups", "adapter", "replica"), "tensor"),
            P("tensor", "replica"),
            P("adapter", "tensor", None),
            P("adapter", None, "tensor"),
            P(("groups", "adapter", "replica"), None),
        ),
        out_specs=P(("groups", "adapter", "replica"), "tensor"),
        check_vma=False,
    )
```

```python
import functools

import jax
import jax.numpy as jnp
from jax import lax
from jax.experimental import pallas as pl
from jax.experimental.pallas import tpu as pltpu
from jax.sharding import PartitionSpec as P

F32 = jnp.float32
BF16 = jnp.bfloat16
VMEM = pl.BlockSpec(memory_space=pltpu.VMEM)
SMEM = pl.BlockSpec(memory_space=pltpu.SMEM)
HBM = pl.BlockSpec(memory_space=pltpu.HBM)
CHUNKS = 4
BATCH = 4


def call(kernel, outs, args, scratch=(), flops=0, limit=16, specs=None):
    size = sum(a.size * a.dtype.itemsize for a in args)
    return pl.pallas_call(
        kernel,
        out_shape=outs,
        in_specs=specs or [VMEM] * len(args),
        out_specs=jax.tree.map(lambda _: VMEM, outs),
        scratch_shapes=scratch,
        compiler_params=pltpu.CompilerParams(vmem_limit_bytes=limit << 20),
        cost_estimate=pl.CostEstimate(flops=flops, bytes_accessed=size, transcendentals=0),
    )(*args)


def chunks(refs, buffers, sems):
    copies = []
    for k in range(CHUNKS):
        copies.append([])
        for n, (ref, buffer) in enumerate(zip(refs, buffers)):
            copy = pltpu.make_async_copy(ref(k), buffer.at[k], sems.at[n, k])
            copy.start()
            copies[-1].append(copy)
    return copies


def part(ref, axis):
    size = ref.shape[axis] // CHUNKS
    if axis == 0:
        return lambda k: ref.at[pl.ds(k * size, size)]
    return lambda k: ref.at[:, pl.ds(k * size, size)]


def pack_kernel(*refs):
    row = 0
    for ref in refs[:-1]:
        refs[-1][row : row + ref.shape[0], :] = ref[...]
        row += ref.shape[0]


def add_chunk(k, prod, acc, out_ref):
    if k > 0:
        prod = prod + acc[...]
    if k < CHUNKS - 1:
        acc[...] = prod
    else:
        out_ref[...] = prod.astype(BF16)


def first_kernel(x_ref, v_ref, o_ref, x_out, v_buf, acc, sems):
    copies = chunks((part(x_ref, 1), part(v_ref, 0)), (x_out, v_buf), sems)
    for k in range(CHUNKS):
        for copy in copies[k]:
            copy.wait()
        add_chunk(k, jnp.dot(x_out[k], v_buf[k], preferred_element_type=F32), acc, o_ref)


def first_terms(x, v):
    rows, wide, width = x.shape[0], x.shape[1], v.shape[1]
    cut = (CHUNKS, rows, wide // CHUNKS)
    return call(
        first_kernel,
        (jax.ShapeDtypeStruct((rows, width), BF16), jax.ShapeDtypeStruct(cut, BF16)),
        (x, v),
        scratch=[
            pltpu.VMEM((CHUNKS, wide // CHUNKS, width), BF16),
            pltpu.VMEM((rows, width), F32),
            pltpu.SemaphoreType.DMA((2, CHUNKS)),
        ],
        flops=2 * x.size * width,
        limit=48,
        specs=[HBM] * 2,
    )


def next_kernel(x_ref, v_ref, o_ref, v_buf, acc, sems):
    copies = chunks((part(v_ref, 0),), (v_buf,), sems)
    for k in range(CHUNKS):
        copies[k][0].wait()
        add_chunk(k, jnp.dot(x_ref[k], v_buf[k], preferred_element_type=F32), acc, o_ref)


def next_terms(x, v):
    rows, wide, width = x.shape[1], v.shape[0], v.shape[1]
    return call(
        next_kernel,
        jax.ShapeDtypeStruct((rows, width), BF16),
        (x, v),
        scratch=[
            pltpu.VMEM((CHUNKS, wide // CHUNKS, width), BF16),
            pltpu.VMEM((rows, width), F32),
            pltpu.SemaphoreType.DMA((1, CHUNKS)),
        ],
        flops=2 * x.size * width,
        limit=48,
        specs=[VMEM, HBM],
    )


def fill(scratch, refs, pieces, lanes):
    row = 0
    for which, begin, rows in pieces:
        scratch[row : row + rows, :] = refs[which][begin : begin + rows, lanes]
        row += rows


def down_kernel(layout, info_ref, idx_ref, x_ref, own_ref, *refs):
    parts, (low_ref, sent_ref, up_ref, scratch) = refs[:-4], refs[-4:]
    rank, size, cols = low_ref.shape[0], x_ref.shape[2], own_ref.shape[1]
    up_ref[:rank, :] = own_ref[...]
    pieces = [p for pieces in layout[1:] for p in pieces]
    fill(up_ref.at[rank:], parts, pieces, slice(CHUNKS * size, CHUNKS * size + cols))
    low = jnp.zeros(low_ref.shape, F32)
    for first in range(0, len(layout), BATCH):
        group = layout[first : first + BATCH]
        prod = 0.0
        for k in range(CHUNKS):
            lanes = slice(k * size, (k + 1) * size)
            fill(scratch.at[k], parts, [p for pieces in group for p in pieces], lanes)
            prod += lax.dot_general(
                scratch[k, : len(group) * rank, :],
                x_ref[k],
                (((1,), (1,)), ((), ())),
                preferred_element_type=F32,
            )
        for k in range(len(group)):
            match = idx_ref[...] == info_ref[first + k]
            low = low + jnp.where(match, prod[k * rank : (k + 1) * rank, :], 0.0)
    low_ref[...] = low
    sent_ref[...] = low.astype(BF16)


def sum_kernel(adapters, info_ref, *refs):
    terms, out_ref = refs[:-1], refs[-1]
    total = jnp.zeros(out_ref.shape, F32)
    for n, term in enumerate(terms):
        total = total + jnp.where(info_ref[adapters + n] == 1, term[...].astype(F32), 0.0)
    out_ref[...] = total


def last_kernel(info_ref, idx_ref, base_ref, up_ref, low_ref, *refs):
    others, (out_ref, spread) = refs[:-2], refs[-2:]
    rank = low_ref.shape[0]
    low = low_ref[...]
    for other in others:
        low = low + other[...].astype(F32)
    low = low.astype(BF16).astype(F32)
    for k in range(up_ref.shape[0] // rank):
        match = idx_ref[...] == info_ref[k]
        spread[k * rank : (k + 1) * rank, :] = jnp.where(match, low, 0.0).astype(BF16)
    lora = lax.dot_general(
        spread[...], up_ref[...], (((0,), (0,)), ((), ())), preferred_element_type=F32
    )
    out_ref[...] = (base_ref[...] + lora.astype(BF16).astype(F32)).astype(BF16)


def after(x, *others):
    return lax.optimization_barrier((x, *others))[0]


def build(mesh):
    groups, adapters = mesh.shape["groups"], mesh.shape["adapter"]
    tensors, replicas = mesh.shape["tensor"], mesh.shape["replica"]

    def shift(x, axis, by):
        size = mesh.shape[axis]
        return lax.ppermute(x, axis, [(i, (i + by) % size) for i in range(size)])

    def others(x, axis):
        return [shift(x, axis, by) for by in range(1, mesh.shape[axis])]

    def flip(x, bits):
        return lax.ppermute(x, "adapter", [(i, i ^ bits) for i in range(adapters)])

    def base_pairs(h, by):
        pairs = {}
        for ti in range(tensors):
            for ri in range(replicas):
                to = (ti + by) % tensors
                if to // per_half == (ri - h) % replicas:
                    pairs[ti * replicas + ri] = to * replicas + ri
        free = set(range(tensors * replicas)) - set(pairs.values())
        for source in range(tensors * replicas):
            if source not in pairs:
                chip = source // replicas
                near = [n for n in sorted(free) if n // replicas == chip] or sorted(free)
                pairs[source] = near[0]
                free.remove(near[0])
        return sorted(pairs.items())

    per_half = max(1, tensors // replicas)

    def shards(x, v, d, u, idx):
        g, a = lax.axis_index("groups"), lax.axis_index("adapter")
        t, r = lax.axis_index("tensor"), lax.axis_index("replica")
        tokens, rank, wide = x.shape[0], d.shape[2], d.shape[1]
        cols = u.shape[2]
        row = idx.reshape(1, tokens)

        order = [*range(1, adapters, 2), *range(2, adapters, 2)]
        halves = [lax.rem(r - h + replicas, replicas) * per_half for h in range(replicas)]
        here = [((t >= n) & (t < n + per_half)).astype(jnp.int32) for n in halves]
        info = [a] + [lax.bitwise_xor(a, jnp.int32(p)) for p in order]
        info = jnp.stack(info + here + [f for f in here for _ in range(1, tensors)])

        held = [v] + others(v, "replica")

        down = d[0].T
        share = rank // (groups * replicas)
        own = jnp.concatenate([down, u[0]], axis=1)
        mine = lax.dynamic_slice_in_dim(own, (g * replicas + r) * share, share, 0)
        near = [p for p in order if p % 2]
        pieces = {p: flip(mine, p) for p in near}

        blocks, recvs = [], []

        def base(h, gate):
            terms, cuts = first_terms(x, v) if h == 0 else (next_terms(xs, held[h]), None)
            half = lax.rem(r - h + replicas, replicas)
            begin = half * per_half

            def cut(n):
                if per_half == 1:
                    return terms
                at = jnp.clip(n - begin, 0, per_half - 1) * cols
                return lax.dynamic_slice_in_dim(terms, at, cols, 1)

            blocks.append(cut(t))
            for by in range(1, tensors):
                block = after(cut(lax.rem(t + by, tensors)), *gate)
                recvs.append(lax.ppermute(block, ("tensor", "replica"), base_pairs(h, by)))
            return terms, cuts

        xs = None
        x, info = lax.optimization_barrier((x, info, mine))[:2]
        first, xs = base(0, [])
        for p, piece in zip(near, lax.optimization_barrier((*[pieces[p] for p in near], first))):
            pieces[p] = piece
        for p in order[len(near) :]:
            pieces[p] = flip(pieces[p + 1], 1)
        for h in range(1, replicas):
            base(h, [])

        arrays, layout = [down], [[(0, 0, rank)]] + [[] for _ in order]

        def keep(array, pair):
            arrays.append(array)
            for n, p in enumerate(pair):
                layout[1 + order.index(p)].append((len(arrays) - 1, n * share, share))

        for n in range(0, len(order), 2):
            pair = order[n : n + 2]
            packed = pieces[pair[0]]
            if len(pair) > 1:
                packed = call(
                    pack_kernel,
                    jax.ShapeDtypeStruct((share * len(pair), wide + cols), BF16),
                    tuple(pieces[p] for p in pair),
                )
            for member in [packed] + others(packed, "groups"):
                keep(member, pair)
                for other in others(member, "replica"):
                    keep(other, pair)

        low, sent, every = call(
            functools.partial(down_kernel, layout),
            (jax.ShapeDtypeStruct((rank, tokens), F32), jax.ShapeDtypeStruct((rank, tokens), BF16),
                jax.ShapeDtypeStruct((adapters * rank, cols), BF16)),
            (info, row, after(xs, *recvs[: tensors - 1]), u[0], *arrays),
            scratch=[
                pltpu.VMEM((CHUNKS, min(BATCH, adapters) * rank, wide // CHUNKS), BF16),
            ],
            flops=2 * x.size * rank * adapters,
            specs=[SMEM] + [VMEM] * (3 + len(arrays)),
        )
        lows = others(sent, "tensor")
        terms = blocks + recvs
        total = call(
            functools.partial(sum_kernel, adapters),
            jax.ShapeDtypeStruct((tokens, cols), F32),
            (info, *terms),
            flops=len(terms) * tokens * cols,
            specs=[SMEM] + [VMEM] * len(terms),
        )
        return call(
            last_kernel,
            jax.ShapeDtypeStruct((tokens, cols), BF16),
            (info, row, total, every, low, *lows),
            scratch=[pltpu.VMEM((adapters * rank, tokens), BF16)],
            flops=2 * tokens * rank * adapters * cols,
            specs=[SMEM] + [VMEM] * (4 + len(lows)),
        )

    return shards


def solution(mesh):
    return jax.shard_map(
        build(mesh),
        mesh=mesh,
        in_specs=(
            P(("groups", "adapter", "replica"), "tensor"),
            P("tensor", "replica"),
            P("adapter", "tensor", None),
            P("adapter", None, "tensor"),
            P(("groups", "adapter", "replica"), None),
        ),
        out_specs=P(("groups", "adapter", "replica"), "tensor"),
        check_vma=False,
    )
```

```python
import functools

import jax
import jax.numpy as jnp
from jax import lax
from jax.experimental import pallas as pl
from jax.experimental.pallas import tpu as pltpu
from jax.sharding import PartitionSpec as P

F32 = jnp.float32
BF16 = jnp.bfloat16
VMEM = pl.BlockSpec(memory_space=pltpu.VMEM)
SMEM = pl.BlockSpec(memory_space=pltpu.SMEM)
HBM = pl.BlockSpec(memory_space=pltpu.HBM)
CHUNKS = 4
BATCH = 4


def call(kernel, outs, args, scratch=(), flops=0, limit=16, specs=None):
    size = sum(a.size * a.dtype.itemsize for a in args)
    return pl.pallas_call(
        kernel,
        out_shape=outs,
        in_specs=specs or [VMEM] * len(args),
        out_specs=jax.tree.map(lambda _: VMEM, outs),
        scratch_shapes=scratch,
        compiler_params=pltpu.CompilerParams(vmem_limit_bytes=limit << 20),
        cost_estimate=pl.CostEstimate(flops=flops, bytes_accessed=size, transcendentals=0),
    )(*args)


def chunks(refs, buffers, sems):
    copies = []
    for k in range(CHUNKS):
        copies.append([])
        for n, (ref, buffer) in enumerate(zip(refs, buffers)):
            copy = pltpu.make_async_copy(ref(k), buffer.at[k], sems.at[n, k])
            copy.start()
            copies[-1].append(copy)
    return copies


def part(ref, axis):
    size = ref.shape[axis] // CHUNKS
    if axis == 0:
        return lambda k: ref.at[pl.ds(k * size, size)]
    return lambda k: ref.at[:, pl.ds(k * size, size)]


def pack_kernel(*refs):
    row = 0
    for ref in refs[:-1]:
        refs[-1][row : row + ref.shape[0], :] = ref[...]
        row += ref.shape[0]


def add_chunk(k, prod, acc, out_ref):
    if k > 0:
        prod = prod + acc[...]
    if k < CHUNKS - 1:
        acc[...] = prod
    else:
        out_ref[...] = prod.astype(BF16)


def first_kernel(x_ref, v_ref, o_ref, x_out, v_buf, acc, sems):
    copies = chunks((part(x_ref, 1), part(v_ref, 0)), (x_out, v_buf), sems)
    for k in range(CHUNKS):
        for copy in copies[k]:
            copy.wait()
        add_chunk(k, jnp.dot(x_out[k], v_buf[k], preferred_element_type=F32), acc, o_ref)


def first_terms(x, v):
    rows, wide, width = x.shape[0], x.shape[1], v.shape[1]
    cut = (CHUNKS, rows, wide // CHUNKS)
    return call(
        first_kernel,
        (jax.ShapeDtypeStruct((rows, width), BF16), jax.ShapeDtypeStruct(cut, BF16)),
        (x, v),
        scratch=[
            pltpu.VMEM((CHUNKS, wide // CHUNKS, width), BF16),
            pltpu.VMEM((rows, width), F32),
            pltpu.SemaphoreType.DMA((2, CHUNKS)),
        ],
        flops=2 * x.size * width,
        limit=48,
        specs=[HBM] * 2,
    )


def next_kernel(x_ref, v_ref, o_ref, v_buf, acc, sems):
    copies = chunks((part(v_ref, 0),), (v_buf,), sems)
    for k in range(CHUNKS):
        copies[k][0].wait()
        add_chunk(k, jnp.dot(x_ref[k], v_buf[k], preferred_element_type=F32), acc, o_ref)


def next_terms(x, v):
    rows, wide, width = x.shape[1], v.shape[0], v.shape[1]
    return call(
        next_kernel,
        jax.ShapeDtypeStruct((rows, width), BF16),
        (x, v),
        scratch=[
            pltpu.VMEM((CHUNKS, wide // CHUNKS, width), BF16),
            pltpu.VMEM((rows, width), F32),
            pltpu.SemaphoreType.DMA((1, CHUNKS)),
        ],
        flops=2 * x.size * width,
        limit=48,
        specs=[VMEM, HBM],
    )


def fill(scratch, refs, pieces, lanes):
    row = 0
    for which, begin, rows in pieces:
        scratch[row : row + rows, :] = refs[which][begin : begin + rows, lanes]
        row += rows


def down_kernel(layout, info_ref, idx_ref, x_ref, own_ref, *refs):
    parts, (low_ref, sent_ref, up_ref, scratch) = refs[:-4], refs[-4:]
    rank, size, cols = low_ref.shape[0], x_ref.shape[2], own_ref.shape[1]
    up_ref[:rank, :] = own_ref[...]
    pieces = [p for pieces in layout[1:] for p in pieces]
    fill(up_ref.at[rank:], parts, pieces, slice(CHUNKS * size, CHUNKS * size + cols))
    low = jnp.zeros(low_ref.shape, F32)
    for first in range(0, len(layout), BATCH):
        group = layout[first : first + BATCH]
        prod = 0.0
        for k in range(CHUNKS):
            lanes = slice(k * size, (k + 1) * size)
            fill(scratch.at[k], parts, [p for pieces in group for p in pieces], lanes)
            prod += lax.dot_general(
                scratch[k, : len(group) * rank, :],
                x_ref[k],
                (((1,), (1,)), ((), ())),
                preferred_element_type=F32,
            )
        for k in range(len(group)):
            match = idx_ref[...] == info_ref[first + k]
            low = low + jnp.where(match, prod[k * rank : (k + 1) * rank, :], 0.0)
    low_ref[...] = low
    sent_ref[...] = low.astype(BF16)


def sum_kernel(adapters, info_ref, *refs):
    terms, out_ref = refs[:-1], refs[-1]
    total = jnp.zeros(out_ref.shape, F32)
    for n, term in enumerate(terms):
        total = total + jnp.where(info_ref[adapters + n] == 1, term[...].astype(F32), 0.0)
    out_ref[...] = total


def last_kernel(info_ref, idx_ref, base_ref, up_ref, low_ref, *refs):
    others, (out_ref, spread) = refs[:-2], refs[-2:]
    rank = low_ref.shape[0]
    low = low_ref[...]
    for other in others:
        low = low + other[...].astype(F32)
    low = low.astype(BF16).astype(F32)
    for k in range(up_ref.shape[0] // rank):
        match = idx_ref[...] == info_ref[k]
        spread[k * rank : (k + 1) * rank, :] = jnp.where(match, low, 0.0).astype(BF16)
    lora = lax.dot_general(
        spread[...], up_ref[...], (((0,), (0,)), ((), ())), preferred_element_type=F32
    )
    out_ref[...] = (base_ref[...] + lora.astype(BF16).astype(F32)).astype(BF16)


def after(x, *others):
    return lax.optimization_barrier((x, *others))[0]


def build(mesh):
    groups, adapters = mesh.shape["groups"], mesh.shape["adapter"]
    tensors, replicas = mesh.shape["tensor"], mesh.shape["replica"]

    def shift(x, axis, by):
        size = mesh.shape[axis]
        return lax.ppermute(x, axis, [(i, (i + by) % size) for i in range(size)])

    def others(x, axis):
        return [shift(x, axis, by) for by in range(1, mesh.shape[axis])]

    def flip(x, bits):
        return lax.ppermute(x, "adapter", [(i, i ^ bits) for i in range(adapters)])

    def base_pairs(h, by):
        pairs = {}
        for ti in range(tensors):
            for ri in range(replicas):
                to = (ti + by) % tensors
                if to // per_half == (ri - h) % replicas:
                    pairs[ti * replicas + ri] = to * replicas + ri
        free = set(range(tensors * replicas)) - set(pairs.values())
        for source in range(tensors * replicas):
            if source not in pairs:
                chip = source // replicas
                near = [n for n in sorted(free) if n // replicas == chip] or sorted(free)
                pairs[source] = near[0]
                free.remove(near[0])
        return sorted(pairs.items())

    per_half = max(1, tensors // replicas)

    def shards(x, v, d, u, idx):
        g, a = lax.axis_index("groups"), lax.axis_index("adapter")
        t, r = lax.axis_index("tensor"), lax.axis_index("replica")
        tokens, rank, wide = x.shape[0], d.shape[2], d.shape[1]
        cols = u.shape[2]
        row = idx.reshape(1, tokens)

        order = [*range(3, adapters, 2), *range(2, adapters, 2), 1][: adapters - 1]
        halves = [lax.rem(r - h + replicas, replicas) * per_half for h in range(replicas)]
        here = [((t >= n) & (t < n + per_half)).astype(jnp.int32) for n in halves]
        info = [a] + [lax.bitwise_xor(a, jnp.int32(p)) for p in order]
        info = jnp.stack(info + here + [f for f in here for _ in range(1, tensors)])

        held = [v] + others(v, "replica")

        down = d[0].T
        share = rank // (groups * replicas)
        own = jnp.concatenate([down, u[0]], axis=1)
        mine, *rest = [
            lax.dynamic_slice_in_dim(
                own, (r * groups + lax.rem(g + n, groups)) * share, share, 0
            )
            for n in range(groups)
        ]
        near = [p for p in order if p % 2 and p > 1]
        pieces = {p: flip(mine, p) for p in near}

        blocks, recvs = [], []

        def base(h, gate):
            terms, cuts = first_terms(x, v) if h == 0 else (next_terms(xs, held[h]), None)
            half = lax.rem(r - h + replicas, replicas)
            begin = half * per_half

            def cut(n):
                if per_half == 1:
                    return terms
                at = jnp.clip(n - begin, 0, per_half - 1) * cols
                return lax.dynamic_slice_in_dim(terms, at, cols, 1)

            blocks.append(cut(t))
            for by in range(1, tensors):
                block = after(cut(lax.rem(t + by, tensors)), *gate)
                recvs.append(lax.ppermute(block, ("tensor", "replica"), base_pairs(h, by)))
            return terms, cuts

        xs = None
        x, info = lax.optimization_barrier((x, info, mine, *rest))[:2]
        first, xs = base(0, [])
        for p, piece in zip(near, lax.optimization_barrier((*[pieces[p] for p in near], first))):
            pieces[p] = piece
        for p in order:
            if p % 2 == 0:
                pieces[p] = flip(pieces[p + 1], 1)
        beside = [flip(after(mine, first), 1)]
        second = first
        for h in range(1, replicas):
            second, _ = base(h, [])
        beside += [flip(after(piece, second), 1) for piece in rest]

        arrays, layout = [down], [[(0, 0, rank)]] + [[] for _ in order]

        def keep(array, p):
            arrays.append(array)
            layout[1 + order.index(p)].append((len(arrays) - 1, 0, array.shape[0]))

        for p in order:
            members = beside if p == 1 else [pieces[p]] + others(pieces[p], "groups")
            if p in [*near, 1] and len(members) > 1:
                shape = (share * groups, wide + cols)
                members = [call(pack_kernel, jax.ShapeDtypeStruct(shape, BF16), tuple(members))]
            for member in members:
                keep(member, p)
                for other in others(member, "replica"):
                    keep(other, p)

        low, sent, every = call(
            functools.partial(down_kernel, layout),
            (jax.ShapeDtypeStruct((rank, tokens), F32), jax.ShapeDtypeStruct((rank, tokens), BF16),
                jax.ShapeDtypeStruct((adapters * rank, cols), BF16)),
            (info, row, after(xs, *recvs[: tensors - 1]), u[0], *arrays),
            scratch=[
                pltpu.VMEM((CHUNKS, min(BATCH, adapters) * rank, wide // CHUNKS), BF16),
            ],
            flops=2 * x.size * rank * adapters,
            specs=[SMEM] + [VMEM] * (3 + len(arrays)),
        )
        lows = others(sent, "tensor")
        terms = blocks + recvs
        total = call(
            functools.partial(sum_kernel, adapters),
            jax.ShapeDtypeStruct((tokens, cols), F32),
            (info, *terms),
            flops=len(terms) * tokens * cols,
            specs=[SMEM] + [VMEM] * len(terms),
        )
        return call(
            last_kernel,
            jax.ShapeDtypeStruct((tokens, cols), BF16),
            (info, row, total, every, low, *lows),
            scratch=[pltpu.VMEM((adapters * rank, tokens), BF16)],
            flops=2 * tokens * rank * adapters * cols,
            specs=[SMEM] + [VMEM] * (4 + len(lows)),
        )

    return shards


def solution(mesh):
    return jax.shard_map(
        build(mesh),
        mesh=mesh,
        in_specs=(
            P(("groups", "adapter", "replica"), "tensor"),
            P("tensor", "replica"),
            P("adapter", "tensor", None),
            P("adapter", None, "tensor"),
            P(("groups", "adapter", "replica"), None),
        ),
        out_specs=P(("groups", "adapter", "replica"), "tensor"),
        check_vma=False,
    )
```

```python
import functools

import jax
import jax.numpy as jnp
from jax import lax
from jax.experimental import pallas as pl
from jax.experimental.pallas import tpu as pltpu
from jax.sharding import PartitionSpec as P

F32 = jnp.float32
BF16 = jnp.bfloat16
VMEM = pl.BlockSpec(memory_space=pltpu.VMEM)
SMEM = pl.BlockSpec(memory_space=pltpu.SMEM)
HBM = pl.BlockSpec(memory_space=pltpu.HBM)
CHUNKS = 4
BATCH = 4


def call(kernel, outs, args, scratch=(), flops=0, limit=16, specs=None):
    size = sum(a.size * a.dtype.itemsize for a in args)
    return pl.pallas_call(
        kernel,
        out_shape=outs,
        in_specs=specs or [VMEM] * len(args),
        out_specs=jax.tree.map(lambda _: VMEM, outs),
        scratch_shapes=scratch,
        compiler_params=pltpu.CompilerParams(vmem_limit_bytes=limit << 20),
        cost_estimate=pl.CostEstimate(flops=flops, bytes_accessed=size, transcendentals=0),
    )(*args)


def chunks(refs, buffers, sems):
    copies = []
    for k in range(CHUNKS):
        copies.append([])
        for n, (ref, buffer) in enumerate(zip(refs, buffers)):
            copy = pltpu.make_async_copy(ref(k), buffer.at[k], sems.at[n, k])
            copy.start()
            copies[-1].append(copy)
    return copies


def part(ref, axis):
    size = ref.shape[axis] // CHUNKS
    if axis == 0:
        return lambda k: ref.at[pl.ds(k * size, size)]
    return lambda k: ref.at[:, pl.ds(k * size, size)]


def pack_kernel(*refs):
    row = 0
    for ref in refs[:-1]:
        refs[-1][row : row + ref.shape[0], :] = ref[...]
        row += ref.shape[0]


def add_chunk(k, prod, acc, out_ref):
    if k > 0:
        prod = prod + acc[...]
    if k < CHUNKS - 1:
        acc[...] = prod
    else:
        out_ref[...] = prod.astype(BF16)


def first_kernel(x_ref, v_ref, o_ref, x_out, v_buf, acc, sems):
    copies = chunks((part(x_ref, 1), part(v_ref, 0)), (x_out, v_buf), sems)
    for k in range(CHUNKS):
        for copy in copies[k]:
            copy.wait()
        add_chunk(k, jnp.dot(x_out[k], v_buf[k], preferred_element_type=F32), acc, o_ref)


def first_terms(x, v):
    rows, wide, width = x.shape[0], x.shape[1], v.shape[1]
    cut = (CHUNKS, rows, wide // CHUNKS)
    return call(
        first_kernel,
        (jax.ShapeDtypeStruct((rows, width), BF16), jax.ShapeDtypeStruct(cut, BF16)),
        (x, v),
        scratch=[
            pltpu.VMEM((CHUNKS, wide // CHUNKS, width), BF16),
            pltpu.VMEM((rows, width), F32),
            pltpu.SemaphoreType.DMA((2, CHUNKS)),
        ],
        flops=2 * x.size * width,
        limit=48,
        specs=[HBM] * 2,
    )


def next_kernel(x_ref, v_ref, o_ref, v_buf, acc, sems):
    copies = chunks((part(v_ref, 0),), (v_buf,), sems)
    for k in range(CHUNKS):
        copies[k][0].wait()
        add_chunk(k, jnp.dot(x_ref[k], v_buf[k], preferred_element_type=F32), acc, o_ref)


def next_terms(x, v):
    rows, wide, width = x.shape[1], v.shape[0], v.shape[1]
    return call(
        next_kernel,
        jax.ShapeDtypeStruct((rows, width), BF16),
        (x, v),
        scratch=[
            pltpu.VMEM((CHUNKS, wide // CHUNKS, width), BF16),
            pltpu.VMEM((rows, width), F32),
            pltpu.SemaphoreType.DMA((1, CHUNKS)),
        ],
        flops=2 * x.size * width,
        limit=48,
        specs=[VMEM, HBM],
    )


def fill(scratch, refs, pieces, lanes):
    row = 0
    for which, begin, rows in pieces:
        scratch[row : row + rows, :] = refs[which][begin : begin + rows, lanes]
        row += rows


def down_kernel(layout, info_ref, idx_ref, x_ref, own_ref, *refs):
    parts, (low_ref, sent_ref, up_ref, scratch) = refs[:-4], refs[-4:]
    rank, size, cols = low_ref.shape[0], x_ref.shape[2], own_ref.shape[1]
    up_ref[:rank, :] = own_ref[...]
    pieces = [p for pieces in layout[1:] for p in pieces]
    fill(up_ref.at[rank:], parts, pieces, slice(CHUNKS * size, CHUNKS * size + cols))
    low = jnp.zeros(low_ref.shape, F32)
    for first in range(0, len(layout), BATCH):
        group = layout[first : first + BATCH]
        prod = 0.0
        for k in range(CHUNKS):
            lanes = slice(k * size, (k + 1) * size)
            fill(scratch.at[k], parts, [p for pieces in group for p in pieces], lanes)
            prod += lax.dot_general(
                scratch[k, : len(group) * rank, :],
                x_ref[k],
                (((1,), (1,)), ((), ())),
                preferred_element_type=F32,
            )
        for k in range(len(group)):
            match = idx_ref[...] == info_ref[first + k]
            low = low + jnp.where(match, prod[k * rank : (k + 1) * rank, :], 0.0)
    low_ref[...] = low
    sent_ref[...] = low.astype(BF16)


def sum_kernel(adapters, info_ref, *refs):
    terms, out_ref = refs[:-1], refs[-1]
    total = jnp.zeros(out_ref.shape, F32)
    for n, term in enumerate(terms):
        total = total + jnp.where(info_ref[adapters + n] == 1, term[...].astype(F32), 0.0)
    out_ref[...] = total


def last_kernel(info_ref, idx_ref, base_ref, up_ref, low_ref, *refs):
    others, (out_ref, spread) = refs[:-2], refs[-2:]
    rank = low_ref.shape[0]
    low = low_ref[...]
    for other in others:
        low = low + other[...].astype(F32)
    low = low.astype(BF16).astype(F32)
    for k in range(up_ref.shape[0] // rank):
        match = idx_ref[...] == info_ref[k]
        spread[k * rank : (k + 1) * rank, :] = jnp.where(match, low, 0.0).astype(BF16)
    lora = lax.dot_general(
        spread[...], up_ref[...], (((0,), (0,)), ((), ())), preferred_element_type=F32
    )
    out_ref[...] = (base_ref[...] + lora.astype(BF16).astype(F32)).astype(BF16)


def after(x, *others):
    return lax.optimization_barrier((x, *others))[0]


def build(mesh):
    groups, adapters = mesh.shape["groups"], mesh.shape["adapter"]
    tensors, replicas = mesh.shape["tensor"], mesh.shape["replica"]

    def shift(x, axis, by):
        size = mesh.shape[axis]
        return lax.ppermute(x, axis, [(i, (i + by) % size) for i in range(size)])

    def others(x, axis):
        return [shift(x, axis, by) for by in range(1, mesh.shape[axis])]

    def flip(x, bits):
        return lax.ppermute(x, "adapter", [(i, i ^ bits) for i in range(adapters)])

    def base_pairs(h, by):
        pairs = {}
        for ti in range(tensors):
            for ri in range(replicas):
                to = (ti + by) % tensors
                if to // per_half == (ri - h) % replicas:
                    pairs[ti * replicas + ri] = to * replicas + ri
        free = set(range(tensors * replicas)) - set(pairs.values())
        for source in range(tensors * replicas):
            if source not in pairs:
                chip = source // replicas
                near = [n for n in sorted(free) if n // replicas == chip] or sorted(free)
                pairs[source] = near[0]
                free.remove(near[0])
        return sorted(pairs.items())

    per_half = max(1, tensors // replicas)

    def shards(x, v, d, u, idx):
        g, a = lax.axis_index("groups"), lax.axis_index("adapter")
        t, r = lax.axis_index("tensor"), lax.axis_index("replica")
        tokens, rank, wide = x.shape[0], d.shape[2], d.shape[1]
        cols = u.shape[2]
        row = idx.reshape(1, tokens)

        order = [*range(3, adapters, 2), *range(2, adapters, 2), 1][: adapters - 1]
        halves = [lax.rem(r - h + replicas, replicas) * per_half for h in range(replicas)]
        here = [((t >= n) & (t < n + per_half)).astype(jnp.int32) for n in halves]
        info = [a] + [lax.bitwise_xor(a, jnp.int32(p)) for p in order]
        info = jnp.stack(info + here + [f for f in here for _ in range(1, tensors)])

        held = [v] + others(v, "replica")

        down = d[0].T
        share = rank // (groups * replicas)
        own = jnp.concatenate([down, u[0]], axis=1)
        mine, *rest = [
            lax.dynamic_slice_in_dim(
                own, (r * groups + lax.rem(g + n, groups)) * share, share, 0
            )
            for n in range(groups)
        ]
        near = [p for p in order if p % 2 and p > 1]
        pieces = {p: flip(mine, p) for p in near}

        blocks, recvs = [], []

        def base(h, gate):
            terms, cuts = first_terms(x, v) if h == 0 else (next_terms(xs, held[h]), None)
            half = lax.rem(r - h + replicas, replicas)
            begin = half * per_half

            def cut(n):
                if per_half == 1:
                    return terms
                at = jnp.clip(n - begin, 0, per_half - 1) * cols
                return lax.dynamic_slice_in_dim(terms, at, cols, 1)

            blocks.append(cut(t))
            for by in range(1, tensors):
                block = after(cut(lax.rem(t + by, tensors)), *gate)
                recvs.append(lax.ppermute(block, ("tensor", "replica"), base_pairs(h, by)))
            return terms, cuts

        xs = None
        x, info = lax.optimization_barrier((x, info, mine, *rest))[:2]
        first, xs = base(0, [])
        for p, piece in zip(near, lax.optimization_barrier((*[pieces[p] for p in near], first))):
            pieces[p] = piece
        for p in order:
            if p % 2 == 0:
                pieces[p] = flip(pieces[p + 1], 1)
        beside = [flip(after(mine, first), 1)]
        second = first
        for h in range(1, replicas):
            second, _ = base(h, [])
        beside += [flip(after(piece, pieces[order[-2]]), 1) for piece in rest]

        arrays, layout = [down], [[(0, 0, rank)]] + [[] for _ in order]

        def keep(array, p):
            arrays.append(array)
            layout[1 + order.index(p)].append((len(arrays) - 1, 0, array.shape[0]))

        for p in order:
            members = beside if p == 1 else [pieces[p]] + others(pieces[p], "groups")
            if p in order and len(members) > 1:
                shape = (share * groups, wide + cols)
                members = [call(pack_kernel, jax.ShapeDtypeStruct(shape, BF16), tuple(members))]
            for member in members:
                keep(member, p)
                for other in others(member, "replica"):
                    keep(other, p)

        low, sent, every = call(
            functools.partial(down_kernel, layout),
            (jax.ShapeDtypeStruct((rank, tokens), F32), jax.ShapeDtypeStruct((rank, tokens), BF16),
                jax.ShapeDtypeStruct((adapters * rank, cols), BF16)),
            (info, row, after(xs, *recvs[: tensors - 1]), u[0], *arrays),
            scratch=[
                pltpu.VMEM((CHUNKS, min(BATCH, adapters) * rank, wide // CHUNKS), BF16),
            ],
            flops=2 * x.size * rank * adapters,
            specs=[SMEM] + [VMEM] * (3 + len(arrays)),
        )
        lows = others(sent, "tensor")
        terms = blocks + recvs
        total = call(
            functools.partial(sum_kernel, adapters),
            jax.ShapeDtypeStruct((tokens, cols), F32),
            (info, *terms),
            flops=len(terms) * tokens * cols,
            specs=[SMEM] + [VMEM] * len(terms),
        )
        return call(
            last_kernel,
            jax.ShapeDtypeStruct((tokens, cols), BF16),
            (info, row, total, every, low, *lows),
            scratch=[pltpu.VMEM((adapters * rank, tokens), BF16)],
            flops=2 * tokens * rank * adapters * cols,
            specs=[SMEM] + [VMEM] * (4 + len(lows)),
        )

    return shards


def solution(mesh):
    return jax.shard_map(
        build(mesh),
        mesh=mesh,
        in_specs=(
            P(("groups", "adapter", "replica"), "tensor"),
            P("tensor", "replica"),
            P("adapter", "tensor", None),
            P("adapter", None, "tensor"),
            P(("groups", "adapter", "replica"), None),
        ),
        out_specs=P(("groups", "adapter", "replica"), "tensor"),
        check_vma=False,
    )
```

```python
import functools

import jax
import jax.numpy as jnp
from jax import lax
from jax.experimental import pallas as pl
from jax.experimental.pallas import tpu as pltpu
from jax.sharding import PartitionSpec as P

F32 = jnp.float32
BF16 = jnp.bfloat16
VMEM = pl.BlockSpec(memory_space=pltpu.VMEM)
SMEM = pl.BlockSpec(memory_space=pltpu.SMEM)
HBM = pl.BlockSpec(memory_space=pltpu.HBM)
CHUNKS = 4
BATCH = 4


def call(kernel, outs, args, scratch=(), flops=0, limit=16, specs=None):
    size = sum(a.size * a.dtype.itemsize for a in args)
    return pl.pallas_call(
        kernel,
        out_shape=outs,
        in_specs=specs or [VMEM] * len(args),
        out_specs=jax.tree.map(lambda _: VMEM, outs),
        scratch_shapes=scratch,
        compiler_params=pltpu.CompilerParams(vmem_limit_bytes=limit << 20),
        cost_estimate=pl.CostEstimate(flops=flops, bytes_accessed=size, transcendentals=0),
    )(*args)


def chunks(refs, buffers, sems):
    copies = []
    for k in range(CHUNKS):
        copies.append([])
        for n, (ref, buffer) in enumerate(zip(refs, buffers)):
            copy = pltpu.make_async_copy(ref(k), buffer.at[k], sems.at[n, k])
            copy.start()
            copies[-1].append(copy)
    return copies


def part(ref, axis):
    size = ref.shape[axis] // CHUNKS
    if axis == 0:
        return lambda k: ref.at[pl.ds(k * size, size)]
    return lambda k: ref.at[:, pl.ds(k * size, size)]


def pack_kernel(*refs):
    row = 0
    for ref in refs[:-1]:
        refs[-1][row : row + ref.shape[0], :] = ref[...]
        row += ref.shape[0]


def add_chunk(k, prod, acc, out_ref):
    if k > 0:
        prod = prod + acc[...]
    if k < CHUNKS - 1:
        acc[...] = prod
    else:
        out_ref[...] = prod.astype(BF16)


def first_kernel(x_ref, v_ref, o_ref, x_out, v_buf, acc, sems):
    copies = chunks((part(x_ref, 1), part(v_ref, 0)), (x_out, v_buf), sems)
    for k in range(CHUNKS):
        for copy in copies[k]:
            copy.wait()
        add_chunk(k, jnp.dot(x_out[k], v_buf[k], preferred_element_type=F32), acc, o_ref)


def first_terms(x, v):
    rows, wide, width = x.shape[0], x.shape[1], v.shape[1]
    cut = (CHUNKS, rows, wide // CHUNKS)
    return call(
        first_kernel,
        (jax.ShapeDtypeStruct((rows, width), BF16), jax.ShapeDtypeStruct(cut, BF16)),
        (x, v),
        scratch=[
            pltpu.VMEM((CHUNKS, wide // CHUNKS, width), BF16),
            pltpu.VMEM((rows, width), F32),
            pltpu.SemaphoreType.DMA((2, CHUNKS)),
        ],
        flops=2 * x.size * width,
        limit=48,
        specs=[HBM] * 2,
    )


def next_kernel(x_ref, v_ref, o_ref, v_buf, acc, sems):
    copies = chunks((part(v_ref, 0),), (v_buf,), sems)
    for k in range(CHUNKS):
        copies[k][0].wait()
        add_chunk(k, jnp.dot(x_ref[k], v_buf[k], preferred_element_type=F32), acc, o_ref)


def next_terms(x, v):
    rows, wide, width = x.shape[1], v.shape[0], v.shape[1]
    return call(
        next_kernel,
        jax.ShapeDtypeStruct((rows, width), BF16),
        (x, v),
        scratch=[
            pltpu.VMEM((CHUNKS, wide // CHUNKS, width), BF16),
            pltpu.VMEM((rows, width), F32),
            pltpu.SemaphoreType.DMA((1, CHUNKS)),
        ],
        flops=2 * x.size * width,
        limit=48,
        specs=[VMEM, HBM],
    )


def fill(scratch, refs, pieces, lanes):
    row = 0
    for which, begin, rows in pieces:
        scratch[row : row + rows, :] = refs[which][begin : begin + rows, lanes]
        row += rows


def down_kernel(layout, slots, slot_ref, x_ref, own_ref, *refs):
    parts, (low_ref, sent_ref, up_ref, scratch) = refs[:-4], refs[-4:]
    rank, size, cols = low_ref.shape[0], x_ref.shape[2], own_ref.shape[1]
    up_ref[:rank, :] = own_ref[...]
    pieces = [p for pieces in layout[1:] for p in pieces]
    fill(up_ref.at[rank:], parts, pieces, slice(CHUNKS * size, CHUNKS * size + cols))
    low = jnp.zeros(low_ref.shape, F32)
    for first in range(0, len(layout), BATCH):
        group = layout[first : first + BATCH]
        prod = 0.0
        for k in range(CHUNKS):
            lanes = slice(k * size, (k + 1) * size)
            fill(scratch.at[k], parts, [p for pieces in group for p in pieces], lanes)
            prod += lax.dot_general(
                scratch[k, : len(group) * rank, :],
                x_ref[k],
                (((1,), (1,)), ((), ())),
                preferred_element_type=F32,
            )
        for k in range(len(group)):
            match = slot_ref[...] == slots[first + k]
            low = low + jnp.where(match, prod[k * rank : (k + 1) * rank, :], 0.0)
    low_ref[...] = low
    sent_ref[...] = low.astype(BF16)


def sum_kernel(flag_ref, *refs):
    terms, out_ref = refs[:-1], refs[-1]
    total = jnp.zeros(out_ref.shape, F32)
    for n, term in enumerate(terms):
        total = total + jnp.where(flag_ref[n] == 1, term[...].astype(F32), 0.0)
    out_ref[...] = total


def last_kernel(slots, slot_ref, base_ref, up_ref, low_ref, *refs):
    others, (out_ref, spread) = refs[:-2], refs[-2:]
    rank = low_ref.shape[0]
    low = low_ref[...]
    for other in others:
        low = low + other[...].astype(F32)
    low = low.astype(BF16).astype(F32)
    for k in range(up_ref.shape[0] // rank):
        match = slot_ref[...] == slots[k]
        spread[k * rank : (k + 1) * rank, :] = jnp.where(match, low, 0.0).astype(BF16)
    lora = lax.dot_general(
        spread[...], up_ref[...], (((0,), (0,)), ((), ())), preferred_element_type=F32
    )
    out_ref[...] = (base_ref[...] + lora.astype(BF16).astype(F32)).astype(BF16)


def after(x, *others):
    return lax.optimization_barrier((x, *others))[0]


def build(mesh):
    groups, adapters = mesh.shape["groups"], mesh.shape["adapter"]
    tensors, replicas = mesh.shape["tensor"], mesh.shape["replica"]

    def shift(x, axis, by):
        size = mesh.shape[axis]
        return lax.ppermute(x, axis, [(i, (i + by) % size) for i in range(size)])

    def others(x, axis):
        return [shift(x, axis, by) for by in range(1, mesh.shape[axis])]

    def flip(x, bits):
        return lax.ppermute(x, "adapter", [(i, i ^ bits) for i in range(adapters)])

    def base_pairs(h, by):
        pairs = {}
        for ti in range(tensors):
            for ri in range(replicas):
                to = (ti + by) % tensors
                if to // per_half == (ri - h) % replicas:
                    pairs[ti * replicas + ri] = to * replicas + ri
        free = set(range(tensors * replicas)) - set(pairs.values())
        for source in range(tensors * replicas):
            if source not in pairs:
                chip = source // replicas
                near = [n for n in sorted(free) if n // replicas == chip] or sorted(free)
                pairs[source] = near[0]
                free.remove(near[0])
        return sorted(pairs.items())

    per_half = max(1, tensors // replicas)

    def shards(x, v, d, u, idx):
        g, a = lax.axis_index("groups"), lax.axis_index("adapter")
        t, r = lax.axis_index("tensor"), lax.axis_index("replica")
        tokens, rank, wide = x.shape[0], d.shape[2], d.shape[1]
        cols = u.shape[2]
        row = idx.reshape(1, tokens)

        order = [*range(3, adapters, 2), *range(2, adapters, 2), 1][: adapters - 1]
        halves = [lax.rem(r - h + replicas, replicas) * per_half for h in range(replicas)]
        here = [((t >= n) & (t < n + per_half)).astype(jnp.int32) for n in halves]
        flags = jnp.stack(here + [f for f in here for _ in range(1, tensors)])
        slots = [0, *order]
        slot = lax.bitwise_xor(row, jnp.broadcast_to(a, row.shape))

        held = [v] + others(v, "replica")

        down = d[0].T
        share = rank // (groups * replicas)
        own = jnp.concatenate([down, u[0]], axis=1)
        mine, *rest = [
            lax.dynamic_slice_in_dim(
                own, (r * groups + lax.rem(g + n, groups)) * share, share, 0
            )
            for n in range(groups)
        ]
        near = [p for p in order if p % 2 and p > 1]
        pieces = {p: flip(mine, p) for p in near}

        blocks, recvs = [], []

        def base(h, gate):
            terms, cuts = first_terms(x, v) if h == 0 else (next_terms(xs, held[h]), None)
            half = lax.rem(r - h + replicas, replicas)
            begin = half * per_half

            def cut(n):
                if per_half == 1:
                    return terms
                at = jnp.clip(n - begin, 0, per_half - 1) * cols
                return lax.dynamic_slice_in_dim(terms, at, cols, 1)

            blocks.append(cut(t))
            for by in range(1, tensors):
                block = after(cut(lax.rem(t + by, tensors)), *gate)
                recvs.append(lax.ppermute(block, ("tensor", "replica"), base_pairs(h, by)))
            return terms, cuts

        xs = None
        x, flags, slot = lax.optimization_barrier((x, flags, slot, mine, *rest))[:3]
        first, xs = base(0, [])
        for p, piece in zip(near, lax.optimization_barrier((*[pieces[p] for p in near], first))):
            pieces[p] = piece
        for p in order:
            if p % 2 == 0:
                pieces[p] = flip(pieces[p + 1], 1)
        beside = [flip(after(mine, first), 1)]
        second = first
        for h in range(1, replicas):
            second, _ = base(h, [])
        beside += [flip(after(piece, second), 1) for piece in rest]

        arrays, layout = [down], [[(0, 0, rank)]] + [[] for _ in order]

        def keep(array, p):
            arrays.append(array)
            layout[1 + order.index(p)].append((len(arrays) - 1, 0, array.shape[0]))

        for p in order:
            members = beside if p == 1 else [pieces[p]] + others(pieces[p], "groups")
            if p in [*near, 1] and len(members) > 1:
                shape = (share * groups, wide + cols)
                members = [call(pack_kernel, jax.ShapeDtypeStruct(shape, BF16), tuple(members))]
            for member in members:
                keep(member, p)
                for other in others(member, "replica"):
                    keep(other, p)

        low, sent, every = call(
            functools.partial(down_kernel, layout, slots),
            (jax.ShapeDtypeStruct((rank, tokens), F32), jax.ShapeDtypeStruct((rank, tokens), BF16),
                jax.ShapeDtypeStruct((adapters * rank, cols), BF16)),
            (slot, after(xs, *recvs[: tensors - 1]), u[0], *arrays),
            scratch=[
                pltpu.VMEM((CHUNKS, min(BATCH, adapters) * rank, wide // CHUNKS), BF16),
            ],
            flops=2 * x.size * rank * adapters,
            specs=[VMEM] * (3 + len(arrays)),
        )
        lows = others(sent, "tensor")
        terms = blocks + recvs
        total = call(
            sum_kernel,
            jax.ShapeDtypeStruct((tokens, cols), F32),
            (flags, *terms),
            flops=len(terms) * tokens * cols,
            specs=[SMEM] + [VMEM] * len(terms),
        )
        return call(
            functools.partial(last_kernel, slots),
            jax.ShapeDtypeStruct((tokens, cols), BF16),
            (slot, total, every, low, *lows),
            scratch=[pltpu.VMEM((adapters * rank, tokens), BF16)],
            flops=2 * tokens * rank * adapters * cols,
            specs=[VMEM] * (4 + len(lows)),
        )

    return shards


def solution(mesh):
    return jax.shard_map(
        build(mesh),
        mesh=mesh,
        in_specs=(
            P(("groups", "adapter", "replica"), "tensor"),
            P("tensor", "replica"),
            P("adapter", "tensor", None),
            P("adapter", None, "tensor"),
            P(("groups", "adapter", "replica"), None),
        ),
        out_specs=P(("groups", "adapter", "replica"), "tensor"),
        check_vma=False,
    )
```

```python
import functools

import jax
import jax.numpy as jnp
from jax import lax
from jax.experimental import pallas as pl
from jax.experimental.pallas import tpu as pltpu
from jax.sharding import PartitionSpec as P

F32 = jnp.float32
BF16 = jnp.bfloat16
VMEM = pl.BlockSpec(memory_space=pltpu.VMEM)
SMEM = pl.BlockSpec(memory_space=pltpu.SMEM)
HBM = pl.BlockSpec(memory_space=pltpu.HBM)
CHUNKS = 4
BATCH = 4


def call(kernel, outs, args, scratch=(), flops=0, limit=16, specs=None):
    size = sum(a.size * a.dtype.itemsize for a in args)
    return pl.pallas_call(
        kernel,
        out_shape=outs,
        in_specs=specs or [VMEM] * len(args),
        out_specs=jax.tree.map(lambda _: VMEM, outs),
        scratch_shapes=scratch,
        compiler_params=pltpu.CompilerParams(vmem_limit_bytes=limit << 20),
        cost_estimate=pl.CostEstimate(flops=flops, bytes_accessed=size, transcendentals=0),
    )(*args)


def chunks(refs, buffers, sems):
    copies = []
    for k in range(CHUNKS):
        copies.append([])
        for n, (ref, buffer) in enumerate(zip(refs, buffers)):
            copy = pltpu.make_async_copy(ref(k), buffer.at[k], sems.at[n, k])
            copy.start()
            copies[-1].append(copy)
    return copies


def part(ref, axis):
    size = ref.shape[axis] // CHUNKS
    if axis == 0:
        return lambda k: ref.at[pl.ds(k * size, size)]
    return lambda k: ref.at[:, pl.ds(k * size, size)]


def pack_kernel(*refs):
    row = 0
    for ref in refs[:-1]:
        refs[-1][row : row + ref.shape[0], :] = ref[...]
        row += ref.shape[0]


def add_chunk(k, prod, acc, out_ref):
    if k > 0:
        prod = prod + acc[...]
    if k < CHUNKS - 1:
        acc[...] = prod
    else:
        out_ref[...] = prod.astype(BF16)


def first_kernel(x_ref, v_ref, o_ref, x_out, v_buf, acc, sems):
    copies = chunks((part(x_ref, 1), part(v_ref, 0)), (x_out, v_buf), sems)
    for k in range(CHUNKS):
        for copy in copies[k]:
            copy.wait()
        add_chunk(k, jnp.dot(x_out[k], v_buf[k], preferred_element_type=F32), acc, o_ref)


def first_terms(x, v):
    rows, wide, width = x.shape[0], x.shape[1], v.shape[1]
    cut = (CHUNKS, rows, wide // CHUNKS)
    return call(
        first_kernel,
        (jax.ShapeDtypeStruct((rows, width), BF16), jax.ShapeDtypeStruct(cut, BF16)),
        (x, v),
        scratch=[
            pltpu.VMEM((CHUNKS, wide // CHUNKS, width), BF16),
            pltpu.VMEM((rows, width), F32),
            pltpu.SemaphoreType.DMA((2, CHUNKS)),
        ],
        flops=2 * x.size * width,
        limit=48,
        specs=[HBM] * 2,
    )


def next_kernel(x_ref, v_ref, o_ref, v_buf, acc, sems):
    copies = chunks((part(v_ref, 0),), (v_buf,), sems)
    for k in range(CHUNKS):
        copies[k][0].wait()
        add_chunk(k, jnp.dot(x_ref[k], v_buf[k], preferred_element_type=F32), acc, o_ref)


def next_terms(x, v):
    rows, wide, width = x.shape[1], v.shape[0], v.shape[1]
    return call(
        next_kernel,
        jax.ShapeDtypeStruct((rows, width), BF16),
        (x, v),
        scratch=[
            pltpu.VMEM((CHUNKS, wide // CHUNKS, width), BF16),
            pltpu.VMEM((rows, width), F32),
            pltpu.SemaphoreType.DMA((1, CHUNKS)),
        ],
        flops=2 * x.size * width,
        limit=48,
        specs=[VMEM, HBM],
    )


def fill(scratch, refs, pieces, lanes):
    row = 0
    for which, begin, rows in pieces:
        scratch[row : row + rows, :] = refs[which][begin : begin + rows, lanes]
        row += rows


def down_kernel(layout, slots, idx_ref, own_idx_ref, x_ref, own_ref, *refs):
    parts, (low_ref, sent_ref, up_ref, scratch) = refs[:-4], refs[-4:]
    rank, size, cols = low_ref.shape[0], x_ref.shape[2], own_ref.shape[1]
    up_ref[:rank, :] = own_ref[...]
    pieces = [p for pieces in layout[1:] for p in pieces]
    fill(up_ref.at[rank:], parts, pieces, slice(CHUNKS * size, CHUNKS * size + cols))
    slot = idx_ref[...] ^ own_idx_ref[...]
    low = jnp.zeros(low_ref.shape, F32)
    for first in range(0, len(layout), BATCH):
        group = layout[first : first + BATCH]
        prod = 0.0
        for k in range(CHUNKS):
            lanes = slice(k * size, (k + 1) * size)
            fill(scratch.at[k], parts, [p for pieces in group for p in pieces], lanes)
            prod += lax.dot_general(
                scratch[k, : len(group) * rank, :],
                x_ref[k],
                (((1,), (1,)), ((), ())),
                preferred_element_type=F32,
            )
        for k in range(len(group)):
            match = slot == slots[first + k]
            low = low + jnp.where(match, prod[k * rank : (k + 1) * rank, :], 0.0)
    low_ref[...] = low
    sent_ref[...] = low.astype(BF16)


def sum_kernel(flag_ref, *refs):
    terms, out_ref = refs[:-1], refs[-1]
    total = jnp.zeros(out_ref.shape, F32)
    for n, term in enumerate(terms):
        total = total + jnp.where(flag_ref[n] == 1, term[...].astype(F32), 0.0)
    out_ref[...] = total


def last_kernel(slots, idx_ref, own_idx_ref, base_ref, up_ref, low_ref, *refs):
    others, (out_ref, spread) = refs[:-2], refs[-2:]
    rank = low_ref.shape[0]
    low = low_ref[...]
    for other in others:
        low = low + other[...].astype(F32)
    low = low.astype(BF16).astype(F32)
    slot = idx_ref[...] ^ own_idx_ref[...]
    for k in range(up_ref.shape[0] // rank):
        match = slot == slots[k]
        spread[k * rank : (k + 1) * rank, :] = jnp.where(match, low, 0.0).astype(BF16)
    lora = lax.dot_general(
        spread[...], up_ref[...], (((0,), (0,)), ((), ())), preferred_element_type=F32
    )
    out_ref[...] = (base_ref[...] + lora.astype(BF16).astype(F32)).astype(BF16)


def after(x, *others):
    return lax.optimization_barrier((x, *others))[0]


def build(mesh):
    groups, adapters = mesh.shape["groups"], mesh.shape["adapter"]
    tensors, replicas = mesh.shape["tensor"], mesh.shape["replica"]

    def shift(x, axis, by):
        size = mesh.shape[axis]
        return lax.ppermute(x, axis, [(i, (i + by) % size) for i in range(size)])

    def others(x, axis):
        return [shift(x, axis, by) for by in range(1, mesh.shape[axis])]

    def flip(x, bits):
        return lax.ppermute(x, "adapter", [(i, i ^ bits) for i in range(adapters)])

    def base_pairs(h, by):
        pairs = {}
        for ti in range(tensors):
            for ri in range(replicas):
                to = (ti + by) % tensors
                if to // per_half == (ri - h) % replicas:
                    pairs[ti * replicas + ri] = to * replicas + ri
        free = set(range(tensors * replicas)) - set(pairs.values())
        for source in range(tensors * replicas):
            if source not in pairs:
                chip = source // replicas
                near = [n for n in sorted(free) if n // replicas == chip] or sorted(free)
                pairs[source] = near[0]
                free.remove(near[0])
        return sorted(pairs.items())

    per_half = max(1, tensors // replicas)

    def shards(x, v, d, u, idx):
        g, a = lax.axis_index("groups"), lax.axis_index("adapter")
        t, r = lax.axis_index("tensor"), lax.axis_index("replica")
        tokens, rank, wide = x.shape[0], d.shape[2], d.shape[1]
        cols = u.shape[2]
        row = idx.reshape(1, tokens)

        order = [*range(3, adapters, 2), *range(2, adapters, 2), 1][: adapters - 1]
        halves = [lax.rem(r - h + replicas, replicas) * per_half for h in range(replicas)]
        here = [((t >= n) & (t < n + per_half)).astype(jnp.int32) for n in halves]
        flags = jnp.stack(here + [f for f in here for _ in range(1, tensors)])
        slots = [0, *order]
        own_idx = jnp.broadcast_to(a, row.shape)

        held = [v] + others(v, "replica")

        down = d[0].T
        share = rank // (groups * replicas)
        own = jnp.concatenate([down, u[0]], axis=1)
        mine, *rest = [
            lax.dynamic_slice_in_dim(
                own, (r * groups + lax.rem(g + n, groups)) * share, share, 0
            )
            for n in range(groups)
        ]
        near = [p for p in order if p % 2 and p > 1]
        pieces = {p: flip(mine, p) for p in near}

        blocks, recvs = [], []

        def base(h, gate):
            terms, cuts = first_terms(x, v) if h == 0 else (next_terms(xs, held[h]), None)
            half = lax.rem(r - h + replicas, replicas)
            begin = half * per_half

            def cut(n):
                if per_half == 1:
                    return terms
                at = jnp.clip(n - begin, 0, per_half - 1) * cols
                return lax.dynamic_slice_in_dim(terms, at, cols, 1)

            blocks.append(cut(t))
            for by in range(1, tensors):
                block = after(cut(lax.rem(t + by, tensors)), *gate)
                recvs.append(lax.ppermute(block, ("tensor", "replica"), base_pairs(h, by)))
            return terms, cuts

        xs = None
        x, flags, own_idx = lax.optimization_barrier((x, flags, own_idx, mine, *rest))[:3]
        first, xs = base(0, [])
        for p, piece in zip(near, lax.optimization_barrier((*[pieces[p] for p in near], first))):
            pieces[p] = piece
        for p in order:
            if p % 2 == 0:
                pieces[p] = flip(pieces[p + 1], 1)
        beside = [flip(after(mine, first), 1)]
        second = first
        for h in range(1, replicas):
            second, _ = base(h, [])
        beside += [flip(after(piece, second), 1) for piece in rest]

        arrays, layout = [down], [[(0, 0, rank)]] + [[] for _ in order]

        def keep(array, p):
            arrays.append(array)
            layout[1 + order.index(p)].append((len(arrays) - 1, 0, array.shape[0]))

        for p in order:
            members = beside if p == 1 else [pieces[p]] + others(pieces[p], "groups")
            if p in [*near, 1] and len(members) > 1:
                shape = (share * groups, wide + cols)
                members = [call(pack_kernel, jax.ShapeDtypeStruct(shape, BF16), tuple(members))]
            for member in members:
                keep(member, p)
                for other in others(member, "replica"):
                    keep(other, p)

        low, sent, every = call(
            functools.partial(down_kernel, layout, slots),
            (jax.ShapeDtypeStruct((rank, tokens), F32), jax.ShapeDtypeStruct((rank, tokens), BF16),
                jax.ShapeDtypeStruct((adapters * rank, cols), BF16)),
            (row, own_idx, after(xs, *recvs[: tensors - 1]), u[0], *arrays),
            scratch=[
                pltpu.VMEM((CHUNKS, min(BATCH, adapters) * rank, wide // CHUNKS), BF16),
            ],
            flops=2 * x.size * rank * adapters,
            specs=[VMEM] * (4 + len(arrays)),
        )
        lows = others(sent, "tensor")
        terms = blocks + recvs
        total = call(
            sum_kernel,
            jax.ShapeDtypeStruct((tokens, cols), F32),
            (flags, *terms),
            flops=len(terms) * tokens * cols,
            specs=[SMEM] + [VMEM] * len(terms),
        )
        return call(
            functools.partial(last_kernel, slots),
            jax.ShapeDtypeStruct((tokens, cols), BF16),
            (row, own_idx, total, every, low, *lows),
            scratch=[pltpu.VMEM((adapters * rank, tokens), BF16)],
            flops=2 * tokens * rank * adapters * cols,
            specs=[VMEM] * (5 + len(lows)),
        )

    return shards


def solution(mesh):
    return jax.shard_map(
        build(mesh),
        mesh=mesh,
        in_specs=(
            P(("groups", "adapter", "replica"), "tensor"),
            P("tensor", "replica"),
            P("adapter", "tensor", None),
            P("adapter", None, "tensor"),
            P(("groups", "adapter", "replica"), None),
        ),
        out_specs=P(("groups", "adapter", "replica"), "tensor"),
        check_vma=False,
    )
```

```python
import functools

import jax
import jax.numpy as jnp
from jax import lax
from jax.experimental import pallas as pl
from jax.experimental.pallas import tpu as pltpu
from jax.sharding import PartitionSpec as P

F32 = jnp.float32
BF16 = jnp.bfloat16
VMEM = pl.BlockSpec(memory_space=pltpu.VMEM)
SMEM = pl.BlockSpec(memory_space=pltpu.SMEM)
HBM = pl.BlockSpec(memory_space=pltpu.HBM)
CHUNKS = 4
BATCH = 4


def call(kernel, outs, args, scratch=(), flops=0, limit=16, specs=None):
    size = sum(a.size * a.dtype.itemsize for a in args)
    return pl.pallas_call(
        kernel,
        out_shape=outs,
        in_specs=specs or [VMEM] * len(args),
        out_specs=jax.tree.map(lambda _: VMEM, outs),
        scratch_shapes=scratch,
        compiler_params=pltpu.CompilerParams(vmem_limit_bytes=limit << 20),
        cost_estimate=pl.CostEstimate(flops=flops, bytes_accessed=size, transcendentals=0),
    )(*args)


def chunks(refs, buffers, sems):
    copies = []
    for k in range(CHUNKS):
        copies.append([])
        for n, (ref, buffer) in enumerate(zip(refs, buffers)):
            copy = pltpu.make_async_copy(ref(k), buffer.at[k], sems.at[n, k])
            copy.start()
            copies[-1].append(copy)
    return copies


def part(ref, axis):
    size = ref.shape[axis] // CHUNKS
    if axis == 0:
        return lambda k: ref.at[pl.ds(k * size, size)]
    return lambda k: ref.at[:, pl.ds(k * size, size)]


def pack_kernel(*refs):
    row = 0
    for ref in refs[:-1]:
        refs[-1][row : row + ref.shape[0], :] = ref[...]
        row += ref.shape[0]


def add_chunk(k, prod, acc, out_ref):
    if k > 0:
        prod = prod + acc[...]
    if k < CHUNKS - 1:
        acc[...] = prod
    else:
        out_ref[...] = prod.astype(BF16)


def first_kernel(x_ref, v_ref, o_ref, x_out, v_buf, acc, sems):
    copies = chunks((part(x_ref, 1), part(v_ref, 0)), (x_out, v_buf), sems)
    for k in range(CHUNKS):
        for copy in copies[k]:
            copy.wait()
        add_chunk(k, jnp.dot(x_out[k], v_buf[k], preferred_element_type=F32), acc, o_ref)


def first_terms(x, v):
    rows, wide, width = x.shape[0], x.shape[1], v.shape[1]
    cut = (CHUNKS, rows, wide // CHUNKS)
    return call(
        first_kernel,
        (jax.ShapeDtypeStruct((rows, width), BF16), jax.ShapeDtypeStruct(cut, BF16)),
        (x, v),
        scratch=[
            pltpu.VMEM((CHUNKS, wide // CHUNKS, width), BF16),
            pltpu.VMEM((rows, width), F32),
            pltpu.SemaphoreType.DMA((2, CHUNKS)),
        ],
        flops=2 * x.size * width,
        limit=48,
        specs=[HBM] * 2,
    )


def next_kernel(x_ref, v_ref, o_ref, v_buf, acc, sems):
    copies = chunks((part(v_ref, 0),), (v_buf,), sems)
    for k in range(CHUNKS):
        copies[k][0].wait()
        add_chunk(k, jnp.dot(x_ref[k], v_buf[k], preferred_element_type=F32), acc, o_ref)


def next_terms(x, v):
    rows, wide, width = x.shape[1], v.shape[0], v.shape[1]
    return call(
        next_kernel,
        jax.ShapeDtypeStruct((rows, width), BF16),
        (x, v),
        scratch=[
            pltpu.VMEM((CHUNKS, wide // CHUNKS, width), BF16),
            pltpu.VMEM((rows, width), F32),
            pltpu.SemaphoreType.DMA((1, CHUNKS)),
        ],
        flops=2 * x.size * width,
        limit=48,
        specs=[VMEM, HBM],
    )


def fill(scratch, refs, pieces, lanes):
    row = 0
    for which, begin, rows in pieces:
        scratch[row : row + rows, :] = refs[which][begin : begin + rows, lanes]
        row += rows


def down_kernel(layout, slots, idx_ref, own_idx_ref, x_ref, own_ref, *refs):
    parts, (low_ref, sent_ref, up_ref, scratch) = refs[:-4], refs[-4:]
    rank, size, cols = low_ref.shape[0], x_ref.shape[2], own_ref.shape[1]
    up_ref[:rank, :] = own_ref[...]
    pieces = [p for pieces in layout[1:] for p in pieces]
    fill(up_ref.at[rank:], parts, pieces, slice(CHUNKS * size, CHUNKS * size + cols))
    slot = idx_ref[...] ^ own_idx_ref[...]
    low = jnp.zeros(low_ref.shape, F32)
    for first in range(0, len(layout), BATCH):
        group = layout[first : first + BATCH]
        prod = 0.0
        for k in range(CHUNKS):
            lanes = slice(k * size, (k + 1) * size)
            fill(scratch.at[k], parts, [p for pieces in group for p in pieces], lanes)
            prod += lax.dot_general(
                scratch[k, : len(group) * rank, :],
                x_ref[k],
                (((1,), (1,)), ((), ())),
                preferred_element_type=F32,
            )
        for k in range(len(group)):
            match = slot == slots[first + k]
            low = low + jnp.where(match, prod[k * rank : (k + 1) * rank, :], 0.0)
    low_ref[...] = low
    sent_ref[...] = low.astype(BF16)


def sum_kernel(flag_ref, *refs):
    terms, out_ref = refs[:-1], refs[-1]
    total = jnp.zeros(out_ref.shape, F32)
    for n, term in enumerate(terms):
        total = total + jnp.where(flag_ref[n] == 1, term[...].astype(F32), 0.0)
    out_ref[...] = total


def last_kernel(slots, idx_ref, own_idx_ref, base_ref, up_ref, low_ref, *refs):
    others, (out_ref, spread) = refs[:-2], refs[-2:]
    rank = low_ref.shape[0]
    low = low_ref[...]
    for other in others:
        low = low + other[...].astype(F32)
    low = low.astype(BF16).astype(F32)
    slot = idx_ref[...] ^ own_idx_ref[...]
    for k in range(up_ref.shape[0] // rank):
        match = slot == slots[k]
        spread[k * rank : (k + 1) * rank, :] = jnp.where(match, low, 0.0).astype(BF16)
    lora = lax.dot_general(
        spread[...], up_ref[...], (((0,), (0,)), ((), ())), preferred_element_type=F32
    )
    out_ref[...] = (base_ref[...] + lora.astype(BF16).astype(F32)).astype(BF16)


def after(x, *others):
    return lax.optimization_barrier((x, *others))[0]


def build(mesh):
    groups, adapters = mesh.shape["groups"], mesh.shape["adapter"]
    tensors, replicas = mesh.shape["tensor"], mesh.shape["replica"]

    def shift(x, axis, by):
        size = mesh.shape[axis]
        return lax.ppermute(x, axis, [(i, (i + by) % size) for i in range(size)])

    def others(x, axis):
        return [shift(x, axis, by) for by in range(1, mesh.shape[axis])]

    def flip(x, bits):
        return lax.ppermute(x, "adapter", [(i, i ^ bits) for i in range(adapters)])

    def base_pairs(h, by):
        pairs = {}
        for ti in range(tensors):
            for ri in range(replicas):
                to = (ti + by) % tensors
                if to // per_half == (ri - h) % replicas:
                    pairs[ti * replicas + ri] = to * replicas + ri
        free = set(range(tensors * replicas)) - set(pairs.values())
        for source in range(tensors * replicas):
            if source not in pairs:
                chip = source // replicas
                near = [n for n in sorted(free) if n // replicas == chip] or sorted(free)
                pairs[source] = near[0]
                free.remove(near[0])
        return sorted(pairs.items())

    per_half = max(1, tensors // replicas)

    def shards(x, v, d, u, idx):
        g, a = lax.axis_index("groups"), lax.axis_index("adapter")
        t, r = lax.axis_index("tensor"), lax.axis_index("replica")
        tokens, rank, wide = x.shape[0], d.shape[2], d.shape[1]
        cols = u.shape[2]
        row = idx.reshape(1, tokens)

        order = [*range(3, adapters, 2), *range(2, adapters, 2), 1][: adapters - 1]
        halves = [lax.rem(r - h + replicas, replicas) * per_half for h in range(replicas)]
        here = [((t >= n) & (t < n + per_half)).astype(jnp.int32) for n in halves]
        flags = jnp.stack(here + [f for f in here for _ in range(1, tensors)])
        slots = [0, *order]
        own_idx = jnp.broadcast_to(a, row.shape)

        held = [v] + others(v, "replica")

        down = d[0].T
        share = rank // (groups * replicas)
        own = jnp.concatenate([down, u[0]], axis=1)
        mine, *rest = [
            lax.dynamic_slice_in_dim(
                own, (r * groups + lax.rem(g + n, groups)) * share, share, 0
            )
            for n in range(groups)
        ]
        near = [p for p in order if p % 2 and p > 1]
        pieces = {p: flip(mine, p) for p in near}

        blocks, recvs = [], []

        def base(h, gate):
            terms, cuts = first_terms(x, v) if h == 0 else (next_terms(xs, held[h]), None)
            half = lax.rem(r - h + replicas, replicas)
            begin = half * per_half

            def cut(n):
                if per_half == 1:
                    return terms
                at = jnp.clip(n - begin, 0, per_half - 1) * cols
                return lax.dynamic_slice_in_dim(terms, at, cols, 1)

            blocks.append(cut(t))
            for by in range(1, tensors):
                block = after(cut(lax.rem(t + by, tensors)), *gate)
                recvs.append(lax.ppermute(block, ("tensor", "replica"), base_pairs(h, by)))
            return terms, cuts

        xs = None
        x, flags, own_idx = lax.optimization_barrier((x, flags, own_idx, mine, *rest))[:3]
        first, xs = base(0, [])
        for p, piece in zip(near, lax.optimization_barrier((*[pieces[p] for p in near], first))):
            pieces[p] = piece
        for p in order:
            if p % 2 == 0:
                pieces[p] = flip(pieces[p + 1], 1)
        beside = [flip(after(mine, first), 1)]
        second = first
        for h in range(1, replicas):
            second, _ = base(h, [beside[0], *pieces.values()])
        beside += [flip(after(piece, second), 1) for piece in rest]

        arrays, layout = [down], [[(0, 0, rank)]] + [[] for _ in order]

        def keep(array, p):
            arrays.append(array)
            layout[1 + order.index(p)].append((len(arrays) - 1, 0, array.shape[0]))

        for p in order:
            members = beside if p == 1 else [pieces[p]] + others(pieces[p], "groups")
            if p in [*near, 1] and len(members) > 1:
                shape = (share * groups, wide + cols)
                members = [call(pack_kernel, jax.ShapeDtypeStruct(shape, BF16), tuple(members))]
            for member in members:
                keep(member, p)
                for other in others(member, "replica"):
                    keep(other, p)

        low, sent, every = call(
            functools.partial(down_kernel, layout, slots),
            (jax.ShapeDtypeStruct((rank, tokens), F32), jax.ShapeDtypeStruct((rank, tokens), BF16),
                jax.ShapeDtypeStruct((adapters * rank, cols), BF16)),
            (row, own_idx, after(xs, *recvs[: tensors - 1]), u[0], *arrays),
            scratch=[
                pltpu.VMEM((CHUNKS, min(BATCH, adapters) * rank, wide // CHUNKS), BF16),
            ],
            flops=2 * x.size * rank * adapters,
            specs=[VMEM] * (4 + len(arrays)),
        )
        lows = others(sent, "tensor")
        terms = blocks + recvs
        total = call(
            sum_kernel,
            jax.ShapeDtypeStruct((tokens, cols), F32),
            (flags, *terms),
            flops=len(terms) * tokens * cols,
            specs=[SMEM] + [VMEM] * len(terms),
        )
        return call(
            functools.partial(last_kernel, slots),
            jax.ShapeDtypeStruct((tokens, cols), BF16),
            (row, own_idx, total, every, low, *lows),
            scratch=[pltpu.VMEM((adapters * rank, tokens), BF16)],
            flops=2 * tokens * rank * adapters * cols,
            specs=[VMEM] * (5 + len(lows)),
        )

    return shards


def solution(mesh):
    return jax.shard_map(
        build(mesh),
        mesh=mesh,
        in_specs=(
            P(("groups", "adapter", "replica"), "tensor"),
            P("tensor", "replica"),
            P("adapter", "tensor", None),
            P("adapter", None, "tensor"),
            P(("groups", "adapter", "replica"), None),
        ),
        out_specs=P(("groups", "adapter", "replica"), "tensor"),
        check_vma=False,
    )
```

```python
import functools

import jax
import jax.numpy as jnp
from jax import lax
from jax.experimental import pallas as pl
from jax.experimental.pallas import tpu as pltpu
from jax.sharding import PartitionSpec as P

F32 = jnp.float32
BF16 = jnp.bfloat16
VMEM = pl.BlockSpec(memory_space=pltpu.VMEM)
SMEM = pl.BlockSpec(memory_space=pltpu.SMEM)
HBM = pl.BlockSpec(memory_space=pltpu.HBM)
CHUNKS = 4
BATCH = 4


def call(kernel, outs, args, scratch=(), flops=0, limit=16, specs=None):
    size = sum(a.size * a.dtype.itemsize for a in args)
    return pl.pallas_call(
        kernel,
        out_shape=outs,
        in_specs=specs or [VMEM] * len(args),
        out_specs=jax.tree.map(lambda _: VMEM, outs),
        scratch_shapes=scratch,
        compiler_params=pltpu.CompilerParams(vmem_limit_bytes=limit << 20),
        cost_estimate=pl.CostEstimate(flops=flops, bytes_accessed=size, transcendentals=0),
    )(*args)


def chunks(refs, buffers, sems):
    copies = []
    for k in range(CHUNKS):
        copies.append([])
        for n, (ref, buffer) in enumerate(zip(refs, buffers)):
            copy = pltpu.make_async_copy(ref(k), buffer.at[k], sems.at[n, k])
            copy.start()
            copies[-1].append(copy)
    return copies


def part(ref, axis):
    size = ref.shape[axis] // CHUNKS
    if axis == 0:
        return lambda k: ref.at[pl.ds(k * size, size)]
    return lambda k: ref.at[:, pl.ds(k * size, size)]


def pack_kernel(*refs):
    row = 0
    for ref in refs[:-1]:
        refs[-1][row : row + ref.shape[0], :] = ref[...]
        row += ref.shape[0]


def add_chunk(k, prod, acc, out_ref):
    if k > 0:
        prod = prod + acc[...]
    if k < CHUNKS - 1:
        acc[...] = prod
    else:
        out_ref[...] = prod.astype(BF16)


def first_kernel(x_ref, v_ref, o_ref, x_out, v_buf, acc, sems):
    copies = chunks((part(x_ref, 1), part(v_ref, 0)), (x_out, v_buf), sems)
    for k in range(CHUNKS):
        for copy in copies[k]:
            copy.wait()
        add_chunk(k, jnp.dot(x_out[k], v_buf[k], preferred_element_type=F32), acc, o_ref)


def first_terms(x, v):
    rows, wide, width = x.shape[0], x.shape[1], v.shape[1]
    cut = (CHUNKS, rows, wide // CHUNKS)
    return call(
        first_kernel,
        (jax.ShapeDtypeStruct((rows, width), BF16), jax.ShapeDtypeStruct(cut, BF16)),
        (x, v),
        scratch=[
            pltpu.VMEM((CHUNKS, wide // CHUNKS, width), BF16),
            pltpu.VMEM((rows, width), F32),
            pltpu.SemaphoreType.DMA((2, CHUNKS)),
        ],
        flops=2 * x.size * width,
        limit=48,
        specs=[HBM] * 2,
    )


def next_kernel(x_ref, v_ref, o_ref, v_buf, acc, sems):
    copies = chunks((part(v_ref, 0),), (v_buf,), sems)
    for k in range(CHUNKS):
        copies[k][0].wait()
        add_chunk(k, jnp.dot(x_ref[k], v_buf[k], preferred_element_type=F32), acc, o_ref)


def next_terms(x, v):
    rows, wide, width = x.shape[1], v.shape[0], v.shape[1]
    return call(
        next_kernel,
        jax.ShapeDtypeStruct((rows, width), BF16),
        (x, v),
        scratch=[
            pltpu.VMEM((CHUNKS, wide // CHUNKS, width), BF16),
            pltpu.VMEM((rows, width), F32),
            pltpu.SemaphoreType.DMA((1, CHUNKS)),
        ],
        flops=2 * x.size * width,
        limit=48,
        specs=[VMEM, HBM],
    )


def fill(scratch, refs, pieces, lanes):
    row = 0
    for which, begin, rows in pieces:
        scratch[row : row + rows, :] = refs[which][begin : begin + rows, lanes]
        row += rows


def down_kernel(layout, slots, idx_ref, own_idx_ref, x_ref, own_ref, *refs):
    parts, (low_ref, sent_ref, up_ref, scratch) = refs[:-4], refs[-4:]
    rank, size, cols = low_ref.shape[0], x_ref.shape[2], own_ref.shape[1]
    up_ref[:rank, :] = own_ref[...]
    pieces = [p for pieces in layout[1:] for p in pieces]
    fill(up_ref.at[rank:], parts, pieces, slice(CHUNKS * size, CHUNKS * size + cols))
    slot = idx_ref[...] ^ own_idx_ref[...]
    low = jnp.zeros(low_ref.shape, F32)
    for first in range(0, len(layout), BATCH):
        group = layout[first : first + BATCH]
        prod = 0.0
        for k in range(CHUNKS):
            lanes = slice(k * size, (k + 1) * size)
            fill(scratch.at[k], parts, [p for pieces in group for p in pieces], lanes)
            prod += lax.dot_general(
                scratch[k, : len(group) * rank, :],
                x_ref[k],
                (((1,), (1,)), ((), ())),
                preferred_element_type=F32,
            )
        for k in range(len(group)):
            match = slot == slots[first + k]
            low = low + jnp.where(match, prod[k * rank : (k + 1) * rank, :], 0.0)
    low_ref[...] = low
    sent_ref[...] = low.astype(BF16)


def sum_kernel(flag_ref, *refs):
    terms, out_ref = refs[:-1], refs[-1]
    total = jnp.zeros(out_ref.shape, F32)
    for n, term in enumerate(terms):
        total = total + jnp.where(flag_ref[n] == 1, term[...].astype(F32), 0.0)
    out_ref[...] = total


def last_kernel(slots, idx_ref, own_idx_ref, base_ref, up_ref, low_ref, *refs):
    others, (out_ref, spread) = refs[:-2], refs[-2:]
    rank = low_ref.shape[0]
    low = low_ref[...]
    for other in others:
        low = low + other[...].astype(F32)
    low = low.astype(BF16).astype(F32)
    slot = idx_ref[...] ^ own_idx_ref[...]
    for k in range(up_ref.shape[0] // rank):
        match = slot == slots[k]
        spread[k * rank : (k + 1) * rank, :] = jnp.where(match, low, 0.0).astype(BF16)
    lora = lax.dot_general(
        spread[...], up_ref[...], (((0,), (0,)), ((), ())), preferred_element_type=F32
    )
    out_ref[...] = (base_ref[...] + lora.astype(BF16).astype(F32)).astype(BF16)


def after(x, *others):
    return lax.optimization_barrier((x, *others))[0]


def build(mesh):
    groups, adapters = mesh.shape["groups"], mesh.shape["adapter"]
    tensors, replicas = mesh.shape["tensor"], mesh.shape["replica"]

    def shift(x, axis, by):
        size = mesh.shape[axis]
        return lax.ppermute(x, axis, [(i, (i + by) % size) for i in range(size)])

    def others(x, axis):
        return [shift(x, axis, by) for by in range(1, mesh.shape[axis])]

    def flip(x, bits):
        return lax.ppermute(x, "adapter", [(i, i ^ bits) for i in range(adapters)])

    def base_pairs(h, by):
        pairs = {}
        for ti in range(tensors):
            for ri in range(replicas):
                to = (ti + by) % tensors
                if to // per_half == (ri - h) % replicas:
                    pairs[ti * replicas + ri] = to * replicas + ri
        free = set(range(tensors * replicas)) - set(pairs.values())
        for source in range(tensors * replicas):
            if source not in pairs:
                chip = source // replicas
                near = [n for n in sorted(free) if n // replicas == chip] or sorted(free)
                pairs[source] = near[0]
                free.remove(near[0])
        return sorted(pairs.items())

    per_half = max(1, tensors // replicas)

    def shards(x, v, d, u, idx):
        g, a = lax.axis_index("groups"), lax.axis_index("adapter")
        t, r = lax.axis_index("tensor"), lax.axis_index("replica")
        tokens, rank, wide = x.shape[0], d.shape[2], d.shape[1]
        cols = u.shape[2]
        row = idx.reshape(1, tokens)

        order = [*range(3, adapters, 2), *range(2, adapters, 2), 1][: adapters - 1]
        halves = [lax.rem(r - h + replicas, replicas) * per_half for h in range(replicas)]
        here = [((t >= n) & (t < n + per_half)).astype(jnp.int32) for n in halves]
        flags = jnp.stack(here + [f for f in here for _ in range(1, tensors)])
        slots = [0, *order]
        own_idx = jnp.broadcast_to(a, row.shape)

        held = [v] + others(v, "replica")

        down = d[0].T
        share = rank // (groups * replicas)
        own = jnp.concatenate([down, u[0]], axis=1)
        mine, *rest = [
            lax.dynamic_slice_in_dim(
                own, (r * groups + lax.rem(g + n, groups)) * share, share, 0
            )
            for n in range(groups)
        ]
        near = [p for p in order if p % 2 and p > 1]
        pieces = {p: flip(mine, p) for p in near}

        blocks, recvs = [], []

        def base(h, gate):
            terms, cuts = first_terms(x, v) if h == 0 else (next_terms(xs, held[h]), None)
            half = lax.rem(r - h + replicas, replicas)
            begin = half * per_half

            def cut(n):
                if per_half == 1:
                    return terms
                at = jnp.clip(n - begin, 0, per_half - 1) * cols
                return lax.dynamic_slice_in_dim(terms, at, cols, 1)

            blocks.append(cut(t))
            for by in range(1, tensors):
                block = after(cut(lax.rem(t + by, tensors)), *gate)
                recvs.append(lax.ppermute(block, ("tensor", "replica"), base_pairs(h, by)))
            return terms, cuts

        xs = None
        x, flags, own_idx = lax.optimization_barrier((x, flags, own_idx, mine, *rest))[:3]
        first, xs = base(0, [])
        for p, piece in zip(near, lax.optimization_barrier((*[pieces[p] for p in near], first))):
            pieces[p] = piece
        for p in order:
            if p % 2 == 0:
                pieces[p] = flip(pieces[p + 1], 1)
        beside = [flip(after(mine, first), 1)]
        second = first
        for h in range(1, replicas):
            second, _ = base(h, [])
        beside += [flip(after(piece, second), 1) for piece in rest]

        arrays, layout = [down], [[(0, 0, rank)]] + [[] for _ in order]

        def keep(array, p):
            arrays.append(array)
            layout[1 + order.index(p)].append((len(arrays) - 1, 0, array.shape[0]))

        for p in order:
            members = beside if p == 1 else [pieces[p]] + others(pieces[p], "groups")
            if p == 1:
                members = [after(member, *recvs[: tensors - 1]) for member in members]
            if p in [*near, 1] and len(members) > 1:
                shape = (share * groups, wide + cols)
                members = [call(pack_kernel, jax.ShapeDtypeStruct(shape, BF16), tuple(members))]
            for member in members:
                keep(member, p)
                for other in others(member, "replica"):
                    keep(other, p)

        low, sent, every = call(
            functools.partial(down_kernel, layout, slots),
            (jax.ShapeDtypeStruct((rank, tokens), F32), jax.ShapeDtypeStruct((rank, tokens), BF16),
                jax.ShapeDtypeStruct((adapters * rank, cols), BF16)),
            (row, own_idx, after(xs, *recvs[: tensors - 1]), u[0], *arrays),
            scratch=[
                pltpu.VMEM((CHUNKS, min(BATCH, adapters) * rank, wide // CHUNKS), BF16),
            ],
            flops=2 * x.size * rank * adapters,
            specs=[VMEM] * (4 + len(arrays)),
        )
        lows = others(sent, "tensor")
        terms = blocks + recvs
        total = call(
            sum_kernel,
            jax.ShapeDtypeStruct((tokens, cols), F32),
            (flags, *terms),
            flops=len(terms) * tokens * cols,
            specs=[SMEM] + [VMEM] * len(terms),
        )
        return call(
            functools.partial(last_kernel, slots),
            jax.ShapeDtypeStruct((tokens, cols), BF16),
            (row, own_idx, total, every, low, *lows),
            scratch=[pltpu.VMEM((adapters * rank, tokens), BF16)],
            flops=2 * tokens * rank * adapters * cols,
            specs=[VMEM] * (5 + len(lows)),
        )

    return shards


def solution(mesh):
    return jax.shard_map(
        build(mesh),
        mesh=mesh,
        in_specs=(
            P(("groups", "adapter", "replica"), "tensor"),
            P("tensor", "replica"),
            P("adapter", "tensor", None),
            P("adapter", None, "tensor"),
            P(("groups", "adapter", "replica"), None),
        ),
        out_specs=P(("groups", "adapter", "replica"), "tensor"),
        check_vma=False,
    )
```

```python
import functools

import jax
import jax.numpy as jnp
from jax import lax
from jax.experimental import pallas as pl
from jax.experimental.pallas import tpu as pltpu
from jax.sharding import PartitionSpec as P

F32 = jnp.float32
BF16 = jnp.bfloat16
VMEM = pl.BlockSpec(memory_space=pltpu.VMEM)
SMEM = pl.BlockSpec(memory_space=pltpu.SMEM)
HBM = pl.BlockSpec(memory_space=pltpu.HBM)
CHUNKS = 4
BATCH = 4


def call(kernel, outs, args, scratch=(), flops=0, limit=16, specs=None):
    size = sum(a.size * a.dtype.itemsize for a in args)
    return pl.pallas_call(
        kernel,
        out_shape=outs,
        in_specs=specs or [VMEM] * len(args),
        out_specs=jax.tree.map(lambda _: VMEM, outs),
        scratch_shapes=scratch,
        compiler_params=pltpu.CompilerParams(vmem_limit_bytes=limit << 20),
        cost_estimate=pl.CostEstimate(flops=flops, bytes_accessed=size, transcendentals=0),
    )(*args)


def chunks(refs, buffers, sems):
    copies = []
    for k in range(CHUNKS):
        copies.append([])
        for n, (ref, buffer) in enumerate(zip(refs, buffers)):
            copy = pltpu.make_async_copy(ref(k), buffer.at[k], sems.at[n, k])
            copy.start()
            copies[-1].append(copy)
    return copies


def part(ref, axis):
    size = ref.shape[axis] // CHUNKS
    if axis == 0:
        return lambda k: ref.at[pl.ds(k * size, size)]
    return lambda k: ref.at[:, pl.ds(k * size, size)]


def pack_kernel(*refs):
    row = 0
    for ref in refs[:-1]:
        refs[-1][row : row + ref.shape[0], :] = ref[...]
        row += ref.shape[0]


def add_chunk(k, prod, acc, out_ref):
    if k > 0:
        prod = prod + acc[...]
    if k < CHUNKS - 1:
        acc[...] = prod
    else:
        out_ref[...] = prod.astype(BF16)


def first_kernel(x_ref, v_ref, o_ref, x_out, v_buf, acc, sems):
    copies = chunks((part(x_ref, 1), part(v_ref, 0)), (x_out, v_buf), sems)
    for k in range(CHUNKS):
        for copy in copies[k]:
            copy.wait()
        add_chunk(k, jnp.dot(x_out[k], v_buf[k], preferred_element_type=F32), acc, o_ref)


def first_terms(x, v):
    rows, wide, width = x.shape[0], x.shape[1], v.shape[1]
    cut = (CHUNKS, rows, wide // CHUNKS)
    return call(
        first_kernel,
        (jax.ShapeDtypeStruct((rows, width), BF16), jax.ShapeDtypeStruct(cut, BF16)),
        (x, v),
        scratch=[
            pltpu.VMEM((CHUNKS, wide // CHUNKS, width), BF16),
            pltpu.VMEM((rows, width), F32),
            pltpu.SemaphoreType.DMA((2, CHUNKS)),
        ],
        flops=2 * x.size * width,
        limit=48,
        specs=[HBM] * 2,
    )


def next_kernel(x_ref, v_ref, o_ref, v_buf, acc, sems):
    copies = chunks((part(v_ref, 0),), (v_buf,), sems)
    for k in range(CHUNKS):
        copies[k][0].wait()
        add_chunk(k, jnp.dot(x_ref[k], v_buf[k], preferred_element_type=F32), acc, o_ref)


def next_terms(x, v):
    rows, wide, width = x.shape[1], v.shape[0], v.shape[1]
    return call(
        next_kernel,
        jax.ShapeDtypeStruct((rows, width), BF16),
        (x, v),
        scratch=[
            pltpu.VMEM((CHUNKS, wide // CHUNKS, width), BF16),
            pltpu.VMEM((rows, width), F32),
            pltpu.SemaphoreType.DMA((1, CHUNKS)),
        ],
        flops=2 * x.size * width,
        limit=48,
        specs=[VMEM, HBM],
    )


def fill(scratch, refs, pieces, lanes):
    row = 0
    for which, begin, rows in pieces:
        scratch[row : row + rows, :] = refs[which][begin : begin + rows, lanes]
        row += rows


def down_kernel(layout, slots, idx_ref, own_idx_ref, x_ref, own_ref, *refs):
    parts, (low_ref, sent_ref, up_ref, scratch) = refs[:-4], refs[-4:]
    rank, size, cols = low_ref.shape[0], x_ref.shape[2], own_ref.shape[1]
    up_ref[:rank, :] = own_ref[...]
    pieces = [p for pieces in layout[1:] for p in pieces]
    fill(up_ref.at[rank:], parts, pieces, slice(CHUNKS * size, CHUNKS * size + cols))
    slot = idx_ref[...] ^ own_idx_ref[...]
    low = jnp.zeros(low_ref.shape, F32)
    for first in range(0, len(layout), BATCH):
        group = layout[first : first + BATCH]
        prod = 0.0
        for k in range(CHUNKS):
            lanes = slice(k * size, (k + 1) * size)
            fill(scratch.at[k], parts, [p for pieces in group for p in pieces], lanes)
            prod += lax.dot_general(
                scratch[k, : len(group) * rank, :],
                x_ref[k],
                (((1,), (1,)), ((), ())),
                preferred_element_type=F32,
            )
        for k in range(len(group)):
            match = slot == slots[first + k]
            low = low + jnp.where(match, prod[k * rank : (k + 1) * rank, :], 0.0)
    low_ref[...] = low
    sent_ref[...] = low.astype(BF16)


def sum_kernel(flag_ref, *refs):
    terms, out_ref = refs[:-1], refs[-1]
    total = jnp.zeros(out_ref.shape, F32)
    for n, term in enumerate(terms):
        total = total + jnp.where(flag_ref[n] == 1, term[...].astype(F32), 0.0)
    out_ref[...] = total


def last_kernel(slots, idx_ref, own_idx_ref, base_ref, up_ref, low_ref, *refs):
    others, (out_ref, spread) = refs[:-2], refs[-2:]
    rank = low_ref.shape[0]
    low = low_ref[...]
    for other in others:
        low = low + other[...].astype(F32)
    low = low.astype(BF16).astype(F32)
    slot = idx_ref[...] ^ own_idx_ref[...]
    for k in range(up_ref.shape[0] // rank):
        match = slot == slots[k]
        spread[k * rank : (k + 1) * rank, :] = jnp.where(match, low, 0.0).astype(BF16)
    lora = lax.dot_general(
        spread[...], up_ref[...], (((0,), (0,)), ((), ())), preferred_element_type=F32
    )
    out_ref[...] = (base_ref[...] + lora.astype(BF16).astype(F32)).astype(BF16)


def after(x, *others):
    return lax.optimization_barrier((x, *others))[0]


def build(mesh):
    groups, adapters = mesh.shape["groups"], mesh.shape["adapter"]
    tensors, replicas = mesh.shape["tensor"], mesh.shape["replica"]

    def shift(x, axis, by):
        size = mesh.shape[axis]
        return lax.ppermute(x, axis, [(i, (i + by) % size) for i in range(size)])

    def others(x, axis):
        return [shift(x, axis, by) for by in range(1, mesh.shape[axis])]

    def flip(x, bits):
        return lax.ppermute(x, "adapter", [(i, i ^ bits) for i in range(adapters)])

    def base_pairs(h, by):
        pairs = {}
        for ti in range(tensors):
            for ri in range(replicas):
                to = (ti + by) % tensors
                if to // per_half == (ri - h) % replicas:
                    pairs[ti * replicas + ri] = to * replicas + ri
        free = set(range(tensors * replicas)) - set(pairs.values())
        for source in range(tensors * replicas):
            if source not in pairs:
                chip = source // replicas
                near = [n for n in sorted(free) if n // replicas == chip] or sorted(free)
                pairs[source] = near[0]
                free.remove(near[0])
        return sorted(pairs.items())

    per_half = max(1, tensors // replicas)

    def shards(x, v, d, u, idx):
        g, a = lax.axis_index("groups"), lax.axis_index("adapter")
        t, r = lax.axis_index("tensor"), lax.axis_index("replica")
        tokens, rank, wide = x.shape[0], d.shape[2], d.shape[1]
        cols = u.shape[2]
        row = idx.reshape(1, tokens)

        order = [*range(3, adapters, 2), *range(2, adapters, 2), 1][: adapters - 1]
        halves = [lax.rem(r - h + replicas, replicas) * per_half for h in range(replicas)]
        here = [((t >= n) & (t < n + per_half)).astype(jnp.int32) for n in halves]
        flags = jnp.stack(here + [f for f in here for _ in range(1, tensors)])
        slots = [0, *order]
        own_idx = jnp.broadcast_to(a, row.shape)

        held = [v] + others(v, "replica")

        down = d[0].T
        share = rank // (groups * replicas)
        own = jnp.concatenate([down, u[0]], axis=1)
        mine, *rest = [
            lax.dynamic_slice_in_dim(
                own, (r * groups + lax.rem(g + n, groups)) * share, share, 0
            )
            for n in range(groups)
        ]
        near = [p for p in order if p % 2 and p > 1]
        pieces = {p: flip(mine, p) for p in near}

        blocks, recvs = [], []

        def base(h, gate):
            terms, cuts = first_terms(x, v) if h == 0 else (next_terms(xs, held[h]), None)
            half = lax.rem(r - h + replicas, replicas)
            begin = half * per_half

            def cut(n):
                if per_half == 1:
                    return terms
                at = jnp.clip(n - begin, 0, per_half - 1) * cols
                return lax.dynamic_slice_in_dim(terms, at, cols, 1)

            blocks.append(cut(t))
            for by in range(1, tensors):
                block = after(cut(lax.rem(t + by, tensors)), *gate)
                recvs.append(lax.ppermute(block, ("tensor", "replica"), base_pairs(h, by)))
            return terms, cuts

        xs = None
        x, flags, own_idx = lax.optimization_barrier((x, flags, own_idx, mine, *rest))[:3]
        first, xs = base(0, [])
        for p, piece in zip(near, lax.optimization_barrier((*[pieces[p] for p in near], first))):
            pieces[p] = piece
        for p in order:
            if p % 2 == 0:
                pieces[p] = flip(pieces[p + 1], 1)
        beside = [flip(after(mine, first), 1)]
        second = first
        for h in range(1, replicas):
            second, _ = base(h, [])
        beside += [flip(after(piece, *[pieces[p] for p in near]), 1) for piece in rest]

        arrays, layout = [down], [[(0, 0, rank)]] + [[] for _ in order]

        def keep(array, p):
            arrays.append(array)
            layout[1 + order.index(p)].append((len(arrays) - 1, 0, array.shape[0]))

        for p in order:
            members = beside if p == 1 else [pieces[p]] + others(pieces[p], "groups")
            if p in [*near, 1] and len(members) > 1:
                shape = (share * groups, wide + cols)
                members = [call(pack_kernel, jax.ShapeDtypeStruct(shape, BF16), tuple(members))]
            for member in members:
                keep(member, p)
                for other in others(member, "replica"):
                    keep(other, p)

        low, sent, every = call(
            functools.partial(down_kernel, layout, slots),
            (jax.ShapeDtypeStruct((rank, tokens), F32), jax.ShapeDtypeStruct((rank, tokens), BF16),
                jax.ShapeDtypeStruct((adapters * rank, cols), BF16)),
            (row, own_idx, after(xs, *recvs[: tensors - 1]), u[0], *arrays),
            scratch=[
                pltpu.VMEM((CHUNKS, min(BATCH, adapters) * rank, wide // CHUNKS), BF16),
            ],
            flops=2 * x.size * rank * adapters,
            specs=[VMEM] * (4 + len(arrays)),
        )
        lows = others(sent, "tensor")
        terms = blocks + recvs
        total = call(
            sum_kernel,
            jax.ShapeDtypeStruct((tokens, cols), F32),
            (flags, *terms),
            flops=len(terms) * tokens * cols,
            specs=[SMEM] + [VMEM] * len(terms),
        )
        return call(
            functools.partial(last_kernel, slots),
            jax.ShapeDtypeStruct((tokens, cols), BF16),
            (row, own_idx, total, every, low, *lows),
            scratch=[pltpu.VMEM((adapters * rank, tokens), BF16)],
            flops=2 * tokens * rank * adapters * cols,
            specs=[VMEM] * (5 + len(lows)),
        )

    return shards


def solution(mesh):
    return jax.shard_map(
        build(mesh),
        mesh=mesh,
        in_specs=(
            P(("groups", "adapter", "replica"), "tensor"),
            P("tensor", "replica"),
            P("adapter", "tensor", None),
            P("adapter", None, "tensor"),
            P(("groups", "adapter", "replica"), None),
        ),
        out_specs=P(("groups", "adapter", "replica"), "tensor"),
        check_vma=False,
    )
```
